32 devices in a mesh: dp: 16 (over z, y, x), patch: 2 (over core).
Axes of the slice: x: 2, y: 2, z: 4, core: 2. Of those that a mesh axis runs over, the one named last changes fastest.
Arguments:
- embedded_segments: bfloat16 [4608, 64, 128], P(('dp', 'patch')), may hold values from -6 to 6
- history_durations: int32 [4608], P(('dp', 'patch')), may hold values from 336 to 512, as said below
- segment_seen_indicator: int32 [4608, 64], P(('dp', 'patch')), may hold values from 0 to 1, as said below
- query_key_value_matrices: bfloat16 [2, 3, 128, 128], replicated, may hold values from -0.5 to 0.5
- mixing_result_matrices: bfloat16 [2, 128, 128], replicated, may hold values from -1.5 to 1.5
- first_dense_matrices: bfloat16 [2, 128, 256], replicated, may hold values from -0.5 to 0.5
- second_dense_matrices: bfloat16 [2, 256, 128], replicated, may hold values from -0.375 to 0.375
- batchnorm_scales: float32 [2, 2, 128], replicated, may hold values from 0.5 to 1.5
- batchnorm_offsets: float32 [2, 2, 128], replicated, may hold values from -3 to 3
- readout_matrix: bfloat16 [8192, 720], P('patch'), may hold values from -0.0625 to 0.0625
- prediction_cotangent: bfloat16 [4608, 720], P(('dp', 'patch')), may hold values from -6 to 6
Outputs:
- predictions: bfloat16 [4608, 720], P(('dp', 'patch'))
- input_grad: bfloat16 [4608, 64, 128], P(('dp', 'patch'))
- grad_attn_in: float32 [2, 3, 128, 128], replicated
- grad_attn_out: float32 [2, 128, 128], replicated
- grad_up: float32 [2, 128, 256], replicated
- grad_down: float32 [2, 256, 128], replicated
- grad_gain: float32 [2, 2, 128], replicated
- grad_shift: float32 [2, 2, 128], replicated
- grad_head: float32 [8192, 720], P('patch')
The draws below stay inside these ranges and needn't reach their ends.
Inputs may be any that keep to these rules, and one draw needn't show every extreme that they name: `history_durations`: each is 336 or 512. `segment_seen_indicator`: the last patch of every series is observed.
All inputs are finite; a program needn't handle non-finite values.
Results may differ from the reference program's by a relative error of at most 0.028.
The reference program's roundings to bfloat16 on the way count: a program that leaves them out, or rounds other values in their place, can miss the bound.
Values may be sent and summed in bfloat16 or wider, within the bound.
A program may use at most 256 MiB of HBM per device.

```python
import math
import jax
import jax.numpy as jnp
from jax import lax

EMBED_DIMENSION = 128
HEADS = 16
HEAD_DIM = 8
FF = 256
HORIZON_LENGTH = 720
SEGMENT_SLOTS = 64
LAYERS = 2
TOTAL_SIGNALS = 4608


def draw_history_durations(key, part):
    key = jax.random.fold_in(key, 11)
    series_index = jnp.arange(TOTAL_SIGNALS, dtype=jnp.int32)
    threshold = TOTAL_SIGNALS + 2 * series_index
    ticket = jax.random.randint(key, (TOTAL_SIGNALS,), 0, 4 * TOTAL_SIGNALS)
    longer = ticket < threshold
    longer = jnp.where(series_index == 0, True, jnp.where(series_index == 1, False, longer))
    return jnp.where(longer, 512, 336).astype(jnp.int32)


def draw_segment_seen_indicator(key, part):
    key = jax.random.fold_in(key, 23)
    ticket = jax.random.randint(key, (TOTAL_SIGNALS, SEGMENT_SLOTS), 0, 8)
    observed = (ticket < 7).astype(jnp.int32)
    return observed.at[:, SEGMENT_SLOTS - 1].set(1)


def shard_levels(key, extent, pieces, smallest, largest):
    gain = 1.0
    for position, parts in pieces:
        steps = jax.random.uniform(jax.random.fold_in(jax.random.fold_in(key, 6), position), (parts,), jnp.float32, smallest / len(pieces), largest / len(pieces))
        gain = gain * jnp.repeat(jnp.exp(steps), extent[position] // parts).reshape((-1,) + (1,) * (len(extent) - 1 - position))
    return gain


def centred(own_key, extent, scale, most, cuts=(), kind=jnp.bfloat16):
    values = scale * jax.random.normal(own_key, extent, jnp.float32)
    if cuts:
        values = values * shard_levels(own_key, extent, cuts, -0.22, 0.18)
    return jnp.clip(values, -most, most).astype(kind)


def setup_inputs(seed: int = 0) -> dict:
    keys = jax.random.split(jax.random.key(seed), 12)
    return {
        "embedded_segments": centred(keys[0], (TOTAL_SIGNALS, SEGMENT_SLOTS, EMBED_DIMENSION), 1.0, 6.0, ((0, 32),)),
        "history_durations": draw_history_durations(jax.random.fold_in(keys[11], 71), 0),
        "segment_seen_indicator": draw_segment_seen_indicator(jax.random.fold_in(keys[11], 71), 0),
        "query_key_value_matrices": centred(keys[3], (LAYERS, 3, EMBED_DIMENSION, EMBED_DIMENSION), EMBED_DIMENSION ** -0.5, 0.5),
        "mixing_result_matrices": centred(keys[4], (LAYERS, EMBED_DIMENSION, EMBED_DIMENSION), (EMBED_DIMENSION // 8) ** -0.5, 1.5),
        "first_dense_matrices": centred(keys[5], (LAYERS, EMBED_DIMENSION, FF), EMBED_DIMENSION ** -0.5, 0.5),
        "second_dense_matrices": centred(keys[6], (LAYERS, FF, EMBED_DIMENSION), FF ** -0.5, 0.375),
        "batchnorm_scales": jnp.clip(1.0 + 0.1 * jax.random.normal(keys[7], (LAYERS, 2, EMBED_DIMENSION), jnp.float32), 0.5, 1.5),
        "batchnorm_offsets": centred(keys[8], (LAYERS, 2, EMBED_DIMENSION), 0.5, 3.0, (), jnp.float32),
        "readout_matrix": centred(keys[9], (SEGMENT_SLOTS * EMBED_DIMENSION, HORIZON_LENGTH), (SEGMENT_SLOTS * EMBED_DIMENSION) ** -0.5, 0.0625, ((0, 2),)),
        "prediction_cotangent": centred(keys[10], (TOTAL_SIGNALS, HORIZON_LENGTH), 1.0, 6.0, ((0, 32),)),
    }


@jax.custom_vjp
def low(v):
    return lax.optimization_barrier(v.astype(jnp.bfloat16)).astype(jnp.float32)

@jax.custom_vjp
def low_back(v):
    return v

def low_keep(v):
    return (low(v), None)

def low_pass(kept, grad):
    return (grad,)

def back_keep(v):
    return (v, None)

def back_low(kept, grad):
    return (low(grad),)
low.defvjp(low_keep, low_pass)
low_back.defvjp(back_keep, back_low)
HIGHEST_PRECISION = lax.Precision.HIGHEST
norm_eps = 1e-05
filler_score = -1e+30

def blocked(function, arrays):
    block_size = math.gcd(TOTAL_SIGNALS, 64)
    stacked = tuple((member.reshape((TOTAL_SIGNALS // block_size, block_size) + member.shape[1:]) for member in arrays))
    result = lax.map(jax.checkpoint(lambda block_items: function(*block_items)), stacked)
    return result.reshape((TOTAL_SIGNALS,) + result.shape[2:])

def attend_block(rounded, valid_keys, query_weight, key_weight, value_weight, out_weight):
    series_count, patch_count, model_width = rounded.shape

    def heads_of(weight_matrix):
        projected = jnp.einsum('spd,de->spe', rounded, weight_matrix, precision=HIGHEST_PRECISION)
        return low_back(low(projected)).reshape(series_count, patch_count, HEADS, HEAD_DIM)
    queries = heads_of(query_weight)
    key_rows = heads_of(key_weight)
    value_rows = heads_of(value_weight)
    scores = low_back(jnp.einsum('bqhe,bkhe->bhqk', queries, key_rows, precision=HIGHEST_PRECISION) * HEAD_DIM ** (-0.5))
    scores = jnp.where(valid_keys[:, None, None, :] > 0.5, scores, filler_score)
    probabilities = low(jax.nn.softmax(scores, axis=-1))
    mixed_heads = jnp.einsum('bhqk,bkhe->bqhe', probabilities, value_rows, precision=HIGHEST_PRECISION)
    mixed_heads = low_back(low(mixed_heads.reshape(series_count, patch_count, model_width)))
    return low_back(jnp.einsum('spd,de->spe', mixed_heads, out_weight, precision=HIGHEST_PRECISION))

def feed_block(normed, up_weight, down_weight):
    hidden_units = low_back(low(jnp.einsum('spd,df->spf', low(normed), up_weight, precision=HIGHEST_PRECISION)))
    activated = low(jax.nn.gelu(hidden_units))
    return low_back(jnp.einsum('spf,fd->spd', activated, down_weight, precision=HIGHEST_PRECISION))

def batch_norm(values, valid_mask, valid_count, gain_row, shift_row):
    weighted = valid_mask[:, :, None]
    average = lax.optimization_barrier(jnp.sum(weighted * values, axis=(0, 1))) / valid_count
    centered = values - average
    variance = lax.optimization_barrier(jnp.sum(weighted * centered * centered, axis=(0, 1))) / valid_count
    return gain_row * centered * lax.rsqrt(variance + norm_eps) + shift_row

def encoder_forward(inputs, valid_mask, valid_count, query_key_value_matrices, mixing_result_matrices, first_dense_matrices, second_dense_matrices, batchnorm_scales, batchnorm_offsets, readout_matrix):
    hidden_state = inputs
    for layer_index in range(LAYERS):
        weights_in = query_key_value_matrices[layer_index]
        out_weight = mixing_result_matrices[layer_index]
        up_weight = first_dense_matrices[layer_index]
        down_weight = second_dense_matrices[layer_index]
        rounded = low(hidden_state)
        attended = blocked(lambda block_rounded, block_valid: attend_block(block_rounded, block_valid, weights_in[0], weights_in[1], weights_in[2], out_weight), (rounded, valid_mask))
        normed = batch_norm(hidden_state + attended, valid_mask, valid_count, batchnorm_scales[layer_index, 0], batchnorm_offsets[layer_index, 0])
        branch = blocked(lambda block_normed: feed_block(block_normed, up_weight, down_weight), (normed,))
        hidden_state = batch_norm(normed + branch, valid_mask, valid_count, batchnorm_scales[layer_index, 1], batchnorm_offsets[layer_index, 1])
    flattened = low(hidden_state * valid_mask[:, :, None]).reshape(TOTAL_SIGNALS, SEGMENT_SLOTS * EMBED_DIMENSION)
    return jnp.einsum('sr,rh->sh', flattened, readout_matrix, precision=HIGHEST_PRECISION)

def reference(embedded_segments, history_durations, segment_seen_indicator, query_key_value_matrices, mixing_result_matrices, first_dense_matrices, second_dense_matrices, batchnorm_scales, batchnorm_offsets, readout_matrix, prediction_cotangent):
    positions = jnp.arange(SEGMENT_SLOTS, dtype=jnp.int32)
    first_valid = SEGMENT_SLOTS - ((history_durations - 16) // 8 + 2)
    valid_mask = ((positions[None, :] >= first_valid[:, None]) & (segment_seen_indicator > 0)).astype(jnp.float32)
    valid_count = jnp.sum(valid_mask)

    def evaluate_encoder(inputs, weights_in, weight_out, weight_up, weight_down, gains, shifts, weight_head):
        return encoder_forward(inputs, valid_mask, valid_count, weights_in, weight_out, weight_up, weight_down, gains, shifts, weight_head)
    differentiable_operands = (embedded_segments.astype(jnp.float32), query_key_value_matrices.astype(jnp.float32), mixing_result_matrices.astype(jnp.float32), first_dense_matrices.astype(jnp.float32), second_dense_matrices.astype(jnp.float32), batchnorm_scales.astype(jnp.float32), batchnorm_offsets.astype(jnp.float32), readout_matrix.astype(jnp.float32))
    predictions, cotangent_mapper = jax.vjp(evaluate_encoder, *differentiable_operands)
    derivative_nested = cotangent_mapper(prediction_cotangent.astype(jnp.float32))
    return (predictions.astype(jnp.bfloat16), derivative_nested[0].astype(jnp.bfloat16), derivative_nested[1], derivative_nested[2], derivative_nested[3], derivative_nested[4], derivative_nested[5], derivative_nested[6], derivative_nested[7])
```

```python
import functools
import math

import jax
import jax.numpy as jnp
from jax import lax
from jax.experimental import pallas as pl
from jax.experimental.pallas import tpu as pltpu
from jax.sharding import PartitionSpec as P

HEADS = 16
HEAD_DIM = 8
WIDTH = 128
PATCHES = 64
PAIR = 2 * PATCHES
GROUPS = 4
GROUP_ROWS = WIDTH // GROUPS
GROUP_LANES = HEADS // GROUPS * PATCHES
SPREAD = HEADS * PATCHES
EPS = 1e-05
MASKED = -1e30
SCALE = HEAD_DIM**-0.5
SCALE_LOG2 = SCALE * math.log2(math.e)
GELU_IN = math.sqrt(2.0 / math.pi)
GELU_CUBE = 0.044715
CHUNK = 1024
READOUT_CHUNKS = 4
F32 = jnp.float32
BF16 = jnp.bfloat16
VMEM_BYTES = 60 * 2**20


def dot(left, right):
    return lax.dot_general(left, right, (((1,), (0,)), ((), ())), preferred_element_type=F32)


def dot_rows(left, right):
    return lax.dot_general(left, right, (((1,), (1,)), ((), ())), preferred_element_type=F32)


def turn(matrix):
    return matrix.astype(F32).T.astype(matrix.dtype)


def wide(column, lanes):
    return jnp.concatenate([column] * (lanes // WIDTH), axis=1)


def fold_lanes(values):
    total = values[:, :WIDTH]
    for start in range(WIDTH, values.shape[1], WIDTH):
        total = total + values[:, start : start + WIDTH]
    return total


def fold_heads(values):
    return jnp.concatenate([values] * (GROUP_LANES // WIDTH), axis=1)


def side_masks():
    lane = lax.broadcasted_iota(jnp.int32, (WIDTH, PAIR), 1)
    row = lax.broadcasted_iota(jnp.int32, (WIDTH, PAIR), 0)
    left = lane < PATCHES
    even = (row // HEAD_DIM) % 2 == 0
    return left, even


def token_mask(valid):
    return jnp.broadcast_to(valid, (WIDTH, valid.shape[1])).T


def shown_keys(keys, mask):
    parts = []
    for start in range(0, keys.shape[0], PATCHES):
        own = keys[start : start + PATCHES]
        parts.append(jnp.where(mask[start : start + PATCHES] > 0.5, own, own[PATCHES - 1 :]))
    return jnp.concatenate(parts, axis=0)


def spread_pair(tile, left, even, target):
    turned = pltpu.roll(tile, PATCHES, 1)
    keep = left == even
    first = jnp.where(keep, jnp.where(even, tile, turned), 0.0).astype(BF16)
    second = jnp.where(keep, jnp.where(even, turned, tile), 0.0).astype(BF16)
    step = 2 * HEAD_DIM
    for index in range(HEADS // 2):
        rows = slice(index * step, (index + 1) * step)
        lanes = slice(index * PAIR, (index + 1) * PAIR)
        target[0, rows, lanes] = first[rows]
        target[1, rows, lanes] = second[rows]


def halves(tile, left):
    return (
        jnp.where(left, tile, 0.0).astype(BF16),
        jnp.where(left, 0.0, tile).astype(BF16),
    )


def gather_heads(first, second, left):
    parts = []
    for head in range(HEADS // GROUPS):
        rows = slice(head * HEAD_DIM, (head + 1) * HEAD_DIM)
        lanes = slice(head // 2 * PAIR, (head // 2 + 1) * PAIR)
        one, two = first[rows, lanes], second[rows, lanes]
        if head % 2 == 0:
            two = pltpu.roll(two, PATCHES, 1)
        else:
            one = pltpu.roll(one, PATCHES, 1)
        parts.append(jnp.where(left[:HEAD_DIM], one, two))
    return jnp.concatenate(parts, axis=0)


def pair_lanes(pair):
    start = pair * PAIR
    return pl.ds(start if isinstance(start, int) else pl.multiple_of(start, PAIR), PAIR)


def pipeline(pairs, slots, score, soften, mix):
    even, odd = slots
    score(0, even)

    def two_pairs(index, carry):
        first = 2 * index
        mix(jnp.maximum(first - 1, 0), odd)
        score(first + 1, odd)
        soften(first, even)
        mix(first, even)
        score(jnp.minimum(first + 2, pairs - 1), even)
        soften(first + 1, odd)
        return carry

    lax.fori_loop(0, pairs // 2, two_pairs, 0, unroll=True)
    mix(pairs - 1, odd)


def chunks(lanes, work):
    for start in range(0, lanes, CHUNK):
        work(slice(start, start + CHUNK))


def device_at(index, sizes):
    return index // sizes[1], lax.rem(index, sizes[1])


def greet(step, sizes):
    others = sizes[0] * sizes[1]
    own = lax.axis_index("dp") * sizes[1] + lax.axis_index("patch")
    barrier = pltpu.get_barrier_semaphore()

    @pl.when(step == 0)
    def _():
        def signal(offset, carry):
            target = device_at(lax.rem(own + offset, others), sizes)
            pl.semaphore_signal(
                barrier, inc=1, device_id=target, device_id_type=pl.DeviceIdType.MESH
            )
            return carry

        lax.fori_loop(1, others, signal, 0)


def met(sizes):
    pl.semaphore_wait(pltpu.get_barrier_semaphore(), sizes[0] * sizes[1] - 1)


def second_step():
    return jnp.minimum(1, pl.num_programs(0) - 1)


def swap_tiles(sizes, tiles, send, arrive):
    others = sizes[0] * sizes[1]
    own = lax.axis_index("dp") * sizes[1] + lax.axis_index("patch")

    def start(offset, carry):
        pltpu.make_async_remote_copy(
            src_ref=tiles.at[own],
            dst_ref=tiles.at[own],
            send_sem=send,
            recv_sem=arrive,
            device_id=device_at(lax.rem(own + offset, others), sizes),
            device_id_type=pl.DeviceIdType.MESH,
        ).start()
        return carry

    lax.fori_loop(1, others, start, 0)
    await_bytes(tiles.at[pl.ds(0, others - 1)], arrive)
    await_bytes(tiles.at[pl.ds(0, others - 1)], send)


def await_bytes(like, sem):
    pltpu.make_async_copy(like, like, sem).wait()


def readout_copy(source, target, sems):
    return pltpu.make_async_remote_copy(
        src_ref=source,
        dst_ref=target,
        send_sem=sems.at[0],
        recv_sem=sems.at[1],
        device_id=(lax.axis_index("dp"), 1 - lax.axis_index("patch")),
        device_id_type=pl.DeviceIdType.MESH,
    )


def own_part(sizes, inner):
    chip = lax.axis_index("dp")
    return chip // inner, lax.rem(chip, inner) * sizes[1] + lax.axis_index("patch")


def first_patch(sizes, inner, patches, place):
    half = lax.rem(place + lax.axis_index("patch"), sizes[1])
    return (half * inner + place // sizes[1]) * (patches // (inner * sizes[1]))


class Spread:
    def __init__(self, sizes, inner, source, target, like, send, arrive):
        self.sizes, self.inner = sizes, inner
        self.source, self.target, self.like = source, target, like
        self.send, self.arrive = send, arrive
        self.devices = inner * sizes[1]
        self.group, self.own = own_part(sizes, inner)

    def start(self):
        def begin(offset, carry):
            other = lax.rem(self.own + offset, self.devices)
            pltpu.make_async_remote_copy(
                src_ref=self.source(other),
                dst_ref=self.target(self.own),
                send_sem=self.send,
                recv_sem=self.arrive,
                device_id=(
                    self.group * self.inner + other // self.sizes[1],
                    lax.rem(other, self.sizes[1]),
                ),
                device_id_type=pl.DeviceIdType.MESH,
            ).start()
            return carry

        pltpu.make_async_copy(
            self.source(self.own), self.target(self.own), self.arrive
        ).start()
        lax.fori_loop(1, self.devices, begin, 0)

    def receive(self):
        await_bytes(self.like(self.devices), self.arrive)

    def drain(self):
        await_bytes(self.like(self.devices - 1), self.send)

    def finish(self):
        self.receive()
        self.drain()


class Sharing:
    def __init__(self, sizes, inner, whole, source, slots, share, target, sems):
        rows = slots.shape[1]
        self.whole, self.source, self.slots, self.share = whole, source, slots, share

        def part(ref, place):
            return ref.at[pl.ds(pl.multiple_of(place * rows, rows), rows)]

        self.stages = [
            Spread(
                sizes,
                inner,
                lambda place: part(source, place),
                lambda place: slots.at[place],
                lambda count: slots.at[pl.ds(0, count)],
                sems.at[0, 0],
                sems.at[0, 1],
            ),
            Spread(
                sizes,
                inner,
                lambda place: share,
                lambda place: part(target, place),
                lambda count: target.at[pl.ds(0, rows * count)],
                sems.at[1, 0],
                sems.at[1, 1],
            ),
        ]

    def begin(self):
        self.source[...] = self.whole[...].astype(self.source.dtype)
        self.stages[0].start()

    def add(self):
        total = self.slots[0].astype(F32)
        for place in range(1, self.slots.shape[0]):
            total = total + self.slots[place].astype(F32)
        self.share[...] = total.astype(self.share.dtype)


def sharing_dtype(devices):
    return BF16 if 4 * WIDTH // devices % 16 == 0 else F32


def sharing_scratch(devices):
    rows = 4 * WIDTH // devices
    dtype = sharing_dtype(devices)
    return [
        pltpu.VMEM((4 * WIDTH, WIDTH), dtype),
        pltpu.VMEM((devices, rows, WIDTH), dtype),
        pltpu.VMEM((rows, WIDTH), dtype),
        pltpu.SemaphoreType.DMA((2, 2)),
    ]


def ship_rows(sizes, inner, flat, start, slots, send, arrive):
    patches = flat.shape[0]
    part, count = slots.shape[1:3]
    return Spread(
        sizes,
        inner,
        lambda place: flat.at[
            pl.ds(first_patch(sizes, inner, patches, place), part), pl.ds(start, count)
        ],
        lambda slot: slots.at[slot],
        lambda places: slots.at[pl.ds(0, places)],
        send,
        arrive,
    )


def as_columns(row):
    return jnp.broadcast_to(row, (WIDTH, WIDTH)).T


def norm_stats(step, sizes, values, valid, gains, out, scratch):
    pivot, sums, squares, count, tiles, send, arrive = scratch
    lanes = valid.shape[-1]

    @pl.when(step == 0)
    def _():
        own = jnp.sum(valid[...])
        first = jnp.sum(fold_lanes(values[...] * valid[...]), axis=1, keepdims=True) / own
        pivot[...] = jnp.broadcast_to(first, (WIDTH, WIDTH))
        sums[...] = jnp.zeros_like(sums)
        squares[...] = jnp.zeros_like(squares)
        count[...] = jnp.zeros_like(count)

    def add(at):
        centred = (values[:, at] - wide(pivot[...], CHUNK)) * valid[:, at]
        sums[...] += fold_lanes(centred)
        squares[...] += fold_lanes(centred * centred)
        count[...] += jnp.broadcast_to(fold_lanes(valid[:, at]), count.shape)

    chunks(lanes, add)

    @pl.when(step == pl.num_programs(0) - 1)
    def _():
        own = lax.axis_index("dp") * sizes[1] + lax.axis_index("patch")
        total = jnp.broadcast_to(jnp.sum(count[0:1, :]), (1, WIDTH))
        shift = jnp.sum(sums[...].T, axis=0, keepdims=True)
        square = jnp.sum(squares[...].T, axis=0, keepdims=True)
        tiles[own, 0:1, :] = pivot[...].T[0:1, :] + shift / total
        tiles[own, 1:2, :] = square - shift * shift / total
        tiles[own, 2:3, :] = total
        tiles[own, 3:8, :] = jnp.zeros((5, WIDTH), F32)
        swap_tiles(sizes, tiles, send, arrive)
        means, spreads, counts = tiles[:, 0, :], tiles[:, 1, :], tiles[:, 2, :]
        total = jnp.sum(counts, axis=0, keepdims=True)
        mean = jnp.sum(means * counts, axis=0, keepdims=True) / total
        apart = means - mean
        variance = jnp.sum(spreads + counts * (apart * apart), axis=0, keepdims=True) / total
        inverse = lax.rsqrt(variance + EPS)
        out[0] = as_columns(mean)
        out[1] = as_columns(inverse)
        out[2] = as_columns(inverse * gains[0])
        out[3] = as_columns(gains[1])
        out[4] = as_columns(total)
        out[5] = as_columns(gains[0])


def add_gradient(grad, normal, valid, scratch):
    weighted = grad * valid
    scratch[0][...] += fold_lanes(weighted * normal)
    scratch[1][...] += fold_lanes(weighted)


def clear_gradient(step, scratch):
    @pl.when(step == 0)
    def _():
        scratch[0][...] = jnp.zeros_like(scratch[0])
        scratch[1][...] = jnp.zeros_like(scratch[1])


def gradient_sums(step, sizes, columns, columns_out, rows_out, scratch):
    by_normal, plain, tiles, send, arrive = scratch

    @pl.when(step == pl.num_programs(0) - 1)
    def _():
        own = lax.axis_index("dp") * sizes[1] + lax.axis_index("patch")
        tiles[own, 0:1, :] = jnp.sum(by_normal[...].T, axis=0, keepdims=True)
        tiles[own, 1:2, :] = jnp.sum(plain[...].T, axis=0, keepdims=True)
        tiles[own, 2:8, :] = jnp.zeros((6, WIDTH), F32)
        swap_tiles(sizes, tiles, send, arrive)
        summed = jnp.sum(tiles[...], axis=0)
        rows_out[...] = summed
        total = columns[4]
        columns_out[0] = as_columns(summed[0:1, :]) / total
        columns_out[1] = as_columns(summed[1:2, :]) / total


def apply_norm(values, columns):
    lanes = values.shape[1]
    return (values - wide(columns[0], lanes)) * wide(columns[2], lanes) + wide(columns[3], lanes)


def normalise(values, columns):
    lanes = values.shape[1]
    return (values - wide(columns[0], lanes)) * wide(columns[1], lanes)


def back_norm(grad, normal, valid, columns, back_columns):
    lanes = grad.shape[1]
    inner = wide(back_columns[1], lanes) + normal * wide(back_columns[0], lanes)
    return wide(columns[2], lanes) * (grad - valid * inner)


def attention_forward_body(sizes, layer, first_layer, makes_head, *refs):
    if first_layer:
        x_ref, readout, refs = refs[0], refs[1], refs[2:]
        columns = None
    else:
        x_ref, columns, refs = refs[0], refs[1], refs[2:]
    w_in_ref, w_out_ref, valid_ref, scales, offsets = refs[:5]
    refs = refs[5:]
    if makes_head:
        head_refs, refs = refs[:3], refs[3:]
    h_out, qkv_out, o_out, lse_out, columns_out = refs[:5]
    refs = refs[5:]
    if first_layer:
        readout_out, readout_sems = refs[0], refs[-1]
        refs = refs[1:-1]
    if makes_head:
        head_refs, refs = head_refs + refs[:1], refs[1:]
    size = len(FORWARD_SLOT)
    slots, refs = (refs[:size], refs[size : 2 * size]), refs[2 * size :]
    (x_full, q_full, k_rows, tops, sums, w_in, w_out), scratch = refs[:7], refs[7:]
    step = pl.program_id(0)
    greet(step, sizes)

    @pl.when(step == second_step())
    def _():
        met(sizes)
        if first_layer:
            readout_copy(readout, readout_out, readout_sems).start()

    lanes = h_out.shape[-1]
    pairs = lanes // PAIR

    @pl.when(step == 0)
    def _():
        for slot in slots:
            slot[0][...] = jnp.zeros_like(slot[0])
        for part in range(3):
            w_in[part * WIDTH : (part + 1) * WIDTH, :] = turn(w_in_ref[0, part])
        w_out[...] = turn(w_out_ref[0])

    if makes_head:
        head_backward(step, *head_refs)

    def project(at):
        x = x_ref[at, :].astype(F32).T if first_layer else apply_norm(x_ref[0, :, at], columns)
        x_full[:, at] = x
        low = x.astype(BF16)
        q = dot(w_in[0:WIDTH, :], low)
        q_full[:, at] = q
        qkv_out[0, 0:WIDTH, at] = q.astype(BF16)
        k = dot(w_in[WIDTH : 2 * WIDTH, :], low)
        k_rows[at, :] = shown_keys(k.T, token_mask(valid_ref[0, :, at])).astype(BF16)
        qkv_out[0, WIDTH : 2 * WIDTH, at] = k.astype(BF16)
        qkv_out[0, 2 * WIDTH :, at] = dot(w_in[2 * WIDTH :, :], low).astype(BF16)

    chunks(lanes, project)
    left, even = side_masks()

    def score(pair, slot):
        spread, scores, _ = slot
        at = pair_lanes(pair)
        spread_pair(q_full[:, at], left, even, spread)
        keys = k_rows[at, :]
        for side in range(2):
            own = slice(side * PATCHES, (side + 1) * PATCHES)
            for group in range(GROUPS):
                cut = slice(group * GROUP_LANES, (group + 1) * GROUP_LANES)
                scores[own, cut] = dot(keys[own], spread[side, :, cut])

    def soften(pair, slot):
        _, scores, weights = slot
        for side in range(2):
            own = slice(side * PATCHES, (side + 1) * PATCHES)
            for group in range(GROUPS):
                cut = slice(group * GROUP_LANES, (group + 1) * GROUP_LANES)
                shown = scores[own, cut]
                top = jnp.max(shown, axis=0, keepdims=True)
                weights[own, cut] = jnp.exp2((shown - top) * SCALE_LOG2).astype(BF16)
                tops[pl.ds(2 * pair + side, 1), cut] = top

    def mix(pair, slot):
        _, _, weights = slot
        at = pair_lanes(pair)
        valid = valid_ref[0, :, at]
        v_one, v_two = halves(qkv_out[0, 2 * WIDTH :, at].astype(F32) * valid, left)
        ones = jnp.broadcast_to(valid, (HEAD_DIM, PAIR))
        some = left[:HEAD_DIM]
        ones = jnp.concatenate([jnp.where(some, ones, 0.0), jnp.where(some, 0.0, ones)], axis=0)
        ones = ones.astype(BF16)
        for group in range(GROUPS):
            cut = slice(group * GROUP_LANES, (group + 1) * GROUP_LANES)
            rows = slice(group * GROUP_ROWS, (group + 1) * GROUP_ROWS)
            mixed = dot(
                jnp.concatenate([v_one[rows], v_two[rows], ones], axis=0), weights[:, cut]
            )
            products = []
            for side in range(2):
                start = 2 * GROUP_ROWS + side * HEAD_DIM
                total = mixed[start : start + HEAD_DIM]
                sums[pl.ds(2 * pair + side, 1), cut] = total[0:1]
                inverse = jnp.concatenate([1.0 / total] * (GROUP_ROWS // HEAD_DIM), axis=0)
                products.append(mixed[side * GROUP_ROWS : (side + 1) * GROUP_ROWS] * inverse)
            o_out[0, rows, at] = gather_heads(*products, left).astype(BF16)

    pipeline(pairs, slots, score, soften, mix)
    lse_out[0] = tops[...] * SCALE_LOG2 + jnp.log2(sums[...])

    def attend(at):
        h_out[0, :, at] = x_full[:, at] + dot(w_out[...], o_out[0, :, at])

    chunks(lanes, attend)
    if first_layer:

        @pl.when(step == pl.num_programs(0) - 1)
        def _():
            readout_copy(readout, readout_out, readout_sems).wait()

    gains = scales[layer, 0:1, :], offsets[layer, 0:1, :]
    norm_stats(step, sizes, h_out.at[0], valid_ref.at[0], gains, columns_out, scratch)


def feed_forward_body(
    sizes, layer, h_ref, columns, w_up_ref, w_down_ref, valid_ref, scales, offsets,
    f_out, columns_out, w_up, w_down, *scratch,
):
    step = pl.program_id(0)
    greet(step, sizes)

    @pl.when(step == second_step())
    def _():
        met(sizes)

    @pl.when(step == 0)
    def _():
        w_up[...] = turn(w_up_ref[0])
        w_down[...] = turn(w_down_ref[0])

    def feed(at):
        normed = apply_norm(h_ref[0, :, at], columns)
        low = normed.astype(BF16)
        active = []
        for start in range(0, w_up.shape[0], WIDTH):
            u = dot(w_up[start : start + WIDTH, :], low).astype(BF16).astype(F32)
            bent = jnp.tanh(u * (GELU_IN + (GELU_IN * GELU_CUBE) * (u * u)))
            half = 0.5 * u
            active.append((half + half * bent).astype(BF16))
        f_out[0, :, at] = normed + dot(w_down[...], jnp.concatenate(active, axis=0))

    chunks(h_ref.shape[-1], feed)
    gains = scales[layer, 1:2, :], offsets[layer, 1:2, :]
    norm_stats(step, sizes, f_out.at[0], valid_ref.at[0], gains, columns_out, scratch)


def turn_body(
    sizes, f_ref, columns, valid_ref, gz_ref, flat_out, gx_out, back_out, rows_out, turned,
    *scratch,
):
    step = pl.program_id(0)
    patches, block = gz_ref.shape[:2]
    greet(step, sizes)

    @pl.when(step == second_step())
    def _():
        met(sizes)

    clear_gradient(step, scratch)
    shift = lax.axis_index("patch") * (patches // sizes[1])

    def rows_at(patch):
        return pl.ds(lax.rem(patch + shift, patches), block, stride=patches)

    def show(at):
        turned[at, :] = (apply_norm(f_ref[0, :, at], columns) * valid_ref[0, :, at]).T

    def take(at):
        valid = valid_ref[0, :, at]
        grad = turned[at, :].T * valid
        gx_out[0, :, at] = grad
        add_gradient(grad, normalise(f_ref[0, :, at], columns), valid, scratch)

    chunks(f_ref.shape[-1], show)
    for patch in range(patches):
        flat_out[patch] = turned[rows_at(patch), :].astype(BF16)
    for patch in range(patches):
        turned[rows_at(patch), :] = gz_ref[patch]
    chunks(f_ref.shape[-1], take)

    gradient_sums(step, sizes, columns, back_out, rows_out, scratch)


def head_backward(step, cotangent, readout_own, readout_other, out):
    def rows(readout):
        grad = dot(cotangent[...], readout[...])
        for patch in range(out.shape[0]):
            out[patch] = grad[:, patch * WIDTH : (patch + 1) * WIDTH]

    pl.when(step < READOUT_CHUNKS)(lambda: rows(readout_own))
    pl.when((step >= READOUT_CHUNKS) & (step < 2 * READOUT_CHUNKS))(lambda: rows(readout_other))


def head_forward(step, flat, readout_own, readout_other, out, total):
    @pl.when(step == 0)
    def _():
        total[...] = jnp.zeros_like(total)

    def rows(readout):
        for patch in range(0, flat.shape[0], 2):
            pair = jnp.concatenate([flat[patch], flat[patch + 1]], axis=1)
            total[...] += dot_rows(pair, readout[:, patch * WIDTH : (patch + 2) * WIDTH])

    pl.when(step < READOUT_CHUNKS)(lambda: rows(readout_own))
    pl.when((step >= READOUT_CHUNKS) & (step < 2 * READOUT_CHUNKS))(lambda: rows(readout_other))

    @pl.when(step == 2 * READOUT_CHUNKS - 1)
    def _():
        out[...] = total[...].astype(out.dtype)


def head_specs(horizon, half_rows, patches, series):
    chunk = half_rows // READOUT_CHUNKS
    last = 2 * READOUT_CHUNKS - 1
    flat_spec = pl.BlockSpec(
        (chunk // WIDTH, series, WIDTH), lambda step: (jnp.minimum(step, last), 0, 0)
    )
    own_spec = pl.BlockSpec(
        (horizon, chunk), lambda step: (0, jnp.minimum(step, READOUT_CHUNKS - 1))
    )
    other_spec = pl.BlockSpec(
        (horizon, chunk),
        lambda step: (0, jnp.clip(step - READOUT_CHUNKS, 0, READOUT_CHUNKS - 1)),
    )
    return flat_spec, own_spec, other_spec


def head_gradient_body(*refs):
    *parts, cotangent, out, total = refs
    step = pl.program_id(0)

    @pl.when(step == 0)
    def _():
        total[...] = jnp.zeros_like(total)

    sources, part, _, width = parts[0].shape
    start = 0
    for rows in parts:
        count = rows.shape[2]
        right = cotangent[:, start : start + count].reshape(sources * count, -1)
        start += count
        for patch in range(part):
            left = rows[:, patch].reshape(sources * count, width)
            total[patch] += lax.dot_general(
                left, right, (((0,), (0,)), ((), ())), preferred_element_type=F32
            )

    @pl.when(step == pl.num_programs(0) - 1)
    def _():
        for patch in range(part):
            out[:, patch * width : (patch + 1) * width] = total[patch].T.astype(out.dtype)


def widen_body(layers, *refs):
    rows, summed, *tiles = refs[: 2 + 2 * layers]
    out, in_out, out_out, up_out, down_out, gain_out, shift_out = refs[2 + 2 * layers :]
    for at in range(rows.shape[0]):
        width = rows.shape[-1]
        out[:, at * width : (at + 1) * width] = rows[at].astype(out.dtype)

    @pl.when(pl.program_id(0) == 0)
    def _():
        for layer in range(layers):
            attention = 2 * (layers - layer) if layer else 0
            feed = 2 * (layers - layer) - 1
            out_out[layer] = summed[attention, 0:WIDTH, :].astype(F32)
            for part in range(3):
                rows_of_part = slice((part + 1) * WIDTH, (part + 2) * WIDTH)
                in_out[layer, part] = summed[attention, rows_of_part, :].astype(F32)
            up_out[layer, :, :WIDTH] = summed[feed, :WIDTH, :].astype(F32)
            up_out[layer, :, WIDTH:] = summed[feed, WIDTH : 2 * WIDTH, :].astype(F32)
            down_out[layer] = summed[feed, 2 * WIDTH :, :].astype(F32)
            for norm in range(2):
                tile = tiles[2 * layer + norm]
                gain_out[layer, norm : norm + 1, :] = tile[0:1, :]
                shift_out[layer, norm : norm + 1, :] = tile[1:2, :]


def feed_backward_body(sizes, inner, ships, *refs):
    (gx_ref, f_ref, h_ref, columns_two, back_two, columns_one, w_down, w_up,
     valid_ref), refs = refs[:9], refs[9:]
    if ships:
        flat_chunk, readout_own, readout_other, flat, *refs = refs
        gy_out, weights_out, back_out, rows_out, out, slots_out, total, *scratch = refs
        scratch, row_sems = scratch[:-1], scratch[-1]
        rows_sent = ship_rows(sizes, inner, flat, 0, slots_out, row_sems.at[0], row_sems.at[1])
    else:
        gy_out, weights_out, back_out, rows_out, *scratch = refs
    step = pl.program_id(0)
    greet(step, sizes)

    @pl.when(step == second_step())
    def _():
        met(sizes)
        if ships:
            rows_sent.start()

    if ships:
        head_forward(step, flat_chunk, readout_own, readout_other, out, total)
    active_full, low_full, normed_full, units_full, w_up_turned, *scratch = scratch
    clear_gradient(step, scratch)

    @pl.when(step == 0)
    def _():
        weights_out[...] = jnp.zeros_like(weights_out)
        w_up_turned[...] = turn(w_up[0])

    def feed(at):
        valid = valid_ref[0, :, at]
        normed = apply_norm(h_ref[0, :, at], columns_one).astype(BF16)
        normed_full[:, at] = normed
        normal = normalise(f_ref[0, :, at], columns_two)
        grad = back_norm(gx_ref[0, :, at], normal, valid, columns_two, back_two)
        low = grad.astype(BF16)
        low_full[:, at] = low
        grad_units = []
        for start in range(0, w_down.shape[1], WIDTH):
            rows = slice(start, start + WIDTH)
            u = dot(w_up_turned[rows, :], normed).astype(BF16).astype(F32)
            square = u * u
            bent = jnp.tanh(u * (GELU_IN + (GELU_IN * GELU_CUBE) * square))
            half = 0.5 + 0.5 * bent
            active_full[rows, at] = (u * half).astype(BF16)
            inner = (0.5 * GELU_IN) + (1.5 * GELU_IN * GELU_CUBE) * square
            slope = half + (u * inner) * (1.0 - bent * bent)
            grad_units.append((dot(w_down[0, rows, :], low) * slope).astype(BF16))
            units_full[rows, at] = grad_units[-1]
        normal = normalise(h_ref[0, :, at], columns_one)
        grad_normed = grad + dot(w_up[0], jnp.concatenate(grad_units, axis=0))
        gy_out[0, :, at] = grad_normed
        add_gradient(grad_normed, normal, valid, scratch)

    chunks(gx_ref.shape[-1], feed)
    weights_out[2 * WIDTH :, :] += dot_rows(active_full[...], low_full[...])
    by_up = dot_rows(normed_full[...], units_full[...])
    weights_out[0:WIDTH, :] += by_up[:, :WIDTH]
    weights_out[WIDTH : 2 * WIDTH, :] += by_up[:, WIDTH:]
    if ships:
        pl.when(step == pl.num_programs(0) - 1)(rows_sent.finish)
    gradient_sums(step, sizes, columns_one, back_out, rows_out, scratch)


def attention_backward_body(sizes, inner, first_layer, opens, closes, start, *refs):
    (gy_ref, h_ref, qkv_ref, o_ref, lse_ref, valid_ref, columns_one, back_one, w_out, w_in_ref,
     x_ref), refs = refs[:11], refs[11:]
    taken = made = None
    if first_layer:
        ready, (gx_out, summed_out), refs = refs[:3], refs[3:5], refs[5:]
        arrays = 1 + len(ready)
        each = len(sharing_scratch(inner * sizes[1]))
        refs, weights_out, shared = (
            refs[: -1 - each * arrays],
            refs[-1 - each * arrays],
            refs[-each * arrays :],
        )
        shares = []
        for at, whole in enumerate((weights_out,) + tuple(ready)):
            source, slots, share, sems = shared[each * at : each * (at + 1)]
            shares.append(
                Sharing(sizes, inner, whole, source, slots, share, summed_out.at[at], sems)
            )
    else:
        columns_prev, *refs = refs
        if start:
            flat, *refs = refs
        if not opens:
            _, taken, *refs = refs
            taken, made = (taken, refs[0]), None
            refs = refs[1:]
        if closes:
            gx_out, weights_out, back_out, rows_out, *refs = refs
        else:
            gx_out, weights_out, made, *refs = refs
        if start:
            slots_out, *refs, row_sems = refs
            rows_sent = ship_rows(
                sizes, inner, flat, start, slots_out, row_sems.at[0], row_sems.at[1]
            )
        count = len(SUM_SCRATCH) + len(swap_scratch(sizes))
        refs, scratch = refs[:-count], refs[-count:]
    size = len(BACKWARD_SLOT)
    slots = refs[:size], refs[size : 2 * size]
    low_full, grad_full, g_full, k_rows, v_rows, grads, w_in = refs[2 * size :]
    step = pl.program_id(0)
    last = pl.num_programs(0) - 1
    if closes or start:
        greet(step, sizes)

        @pl.when(step == second_step())
        def _():
            met(sizes)
            if first_layer:
                for share in shares[1:]:
                    share.begin()
            elif start:
                rows_sent.start()

    if first_layer:

        @pl.when(step == jnp.maximum(second_step(), last // 2 + 1))
        def _():
            for share in shares[1:]:
                share.stages[0].receive()
                share.add()
                share.stages[1].start()

    lanes = valid_ref.shape[-1]
    pairs = lanes // PAIR

    @pl.when(step == 0)
    def _():
        for slot in slots:
            slot[0][...] = jnp.zeros_like(slot[0])
            slot[1][...] = jnp.zeros_like(slot[1])
        weights_out[...] = jnp.zeros_like(weights_out) if taken is None else taken[0][...]
        for part in range(3):
            w_in[:, part * WIDTH : (part + 1) * WIDTH] = w_in_ref[0, part]

    if not first_layer and taken is None:
        clear_gradient(step, scratch)
    elif not first_layer:

        @pl.when(step == 0)
        def _():
            scratch[0][...] = taken[1][0]
            scratch[1][...] = taken[1][1]

    def prepare(at):
        normal = normalise(h_ref[0, :, at], columns_one)
        grad = back_norm(gy_ref[0, :, at], normal, valid_ref[0, :, at], columns_one, back_one)
        grad_full[:, at] = grad
        low = grad.astype(BF16)
        low_full[:, at] = low
        g_full[:, at] = dot(w_out[0], low).astype(BF16).astype(F32)
        mask = token_mask(valid_ref[0, :, at])
        keys = shown_keys(qkv_ref[0, WIDTH : 2 * WIDTH, at].astype(F32).T, mask)
        k_rows[at, :] = keys.astype(BF16)
        v_rows[at, :] = (qkv_ref[0, 2 * WIDTH :, at].astype(F32).T * mask).astype(BF16)

    chunks(lanes, prepare)
    weights_out[0:WIDTH, :] += dot_rows(o_ref[0], low_full[...])
    left, even = side_masks()

    def score(pair, slot):
        spread_q, spread_g, scores, pulls, _, _, inner = slot
        at = pair_lanes(pair)
        spread_pair(qkv_ref[0, 0:WIDTH, at].astype(F32), left, even, spread_q)
        grad = g_full[:, at]
        spread_pair(grad, left, even, spread_g)
        keys = k_rows[at, :]
        content = v_rows[at, :]
        for side in range(2):
            own = slice(side * PATCHES, (side + 1) * PATCHES)
            for group in range(GROUPS):
                cut = slice(group * GROUP_LANES, (group + 1) * GROUP_LANES)
                scores[own, cut] = dot(keys[own], spread_q[side, :, cut])
                pulls[own, cut] = dot(content[own], spread_g[side, :, cut])
        products = grad * o_ref[0, :, at].astype(F32)
        some = left[:HEAD_DIM]
        for head in range(0, HEADS, 2):
            both = [
                jnp.broadcast_to(
                    jnp.sum(products[start : start + HEAD_DIM], axis=0, keepdims=True),
                    (HEAD_DIM, PAIR),
                )
                for start in (head * HEAD_DIM, (head + 1) * HEAD_DIM)
            ]
            turned = [pltpu.roll(row, PATCHES, 1) for row in both]
            lanes_of = slice(head * PATCHES, (head + 2) * PATCHES)
            inner[0, :, lanes_of] = jnp.where(some, both[0], turned[1])
            inner[1, :, lanes_of] = jnp.where(some, turned[0], both[1])

    def soften(pair, slot):
        _, _, scores, pulls, weights, slopes, inner = slot
        for side in range(2):
            own = slice(side * PATCHES, (side + 1) * PATCHES)
            for group in range(GROUPS):
                cut = slice(group * GROUP_LANES, (group + 1) * GROUP_LANES)
                total = lse_ref[0, pl.ds(2 * pair + side, 1), cut]
                weight = jnp.exp2(scores[own, cut] * SCALE_LOG2 - total)
                weights[own, cut] = weight.astype(BF16)
                mean = jnp.concatenate([inner[side, :, cut]] * (PATCHES // HEAD_DIM), axis=0)
                slopes[own, cut] = (weight * (pulls[own, cut] - mean)).astype(BF16)

    def mix(pair, slot):
        spread_q, spread_g, _, _, weights, slopes, _ = slot
        at = pair_lanes(pair)
        valid = valid_ref[0, :, at]
        k_one, k_two = halves(qkv_ref[0, WIDTH : 2 * WIDTH, at].astype(F32) * valid, left)
        own_left = left[:GROUP_ROWS]
        for group in range(GROUPS):
            cut = slice(group * GROUP_LANES, (group + 1) * GROUP_LANES)
            start = group * GROUP_ROWS
            rows = slice(start, start + GROUP_ROWS)
            weight = weights[:, cut]
            slope = slopes[:, cut]
            by_value = dot_rows(
                jnp.concatenate([spread_g[0, rows, cut], spread_g[1, rows, cut]], axis=0), weight
            )
            by_value = jnp.where(own_left, by_value[:GROUP_ROWS], by_value[GROUP_ROWS:])
            grads[2 * WIDTH + start : 2 * WIDTH + start + GROUP_ROWS, at] = (
                by_value * valid
            ).astype(BF16)
            by_key = dot_rows(
                jnp.concatenate([spread_q[0, rows, cut], spread_q[1, rows, cut]], axis=0), slope
            )
            by_key = jnp.where(own_left, by_key[:GROUP_ROWS], by_key[GROUP_ROWS:])
            grads[WIDTH + start : WIDTH + start + GROUP_ROWS, at] = (
                by_key * (valid * SCALE)
            ).astype(BF16)
            by_query = dot(jnp.concatenate([k_one[rows], k_two[rows]], axis=0), slope)
            grads[rows, at] = (
                gather_heads(by_query[:GROUP_ROWS], by_query[GROUP_ROWS:], left) * SCALE
            ).astype(BF16)

    pipeline(pairs, slots, score, soften, mix)

    def finish(at):
        if first_layer:
            low_full[:, at] = x_ref[at, :].astype(F32).T.astype(BF16)
        else:
            normal = normalise(x_ref[0, :, at], columns_prev)
            inputs = normal * wide(columns_prev[5], CHUNK) + wide(columns_prev[3], CHUNK)
            low_full[:, at] = inputs.astype(BF16)
        grad = grad_full[:, at] + dot(w_in[...], grads[:, at])
        if first_layer:
            gx_out[at, :] = grad.T.astype(BF16)
        else:
            gx_out[0, :, at] = grad
            add_gradient(grad, normal, valid_ref[0, :, at], scratch)

    chunks(lanes, finish)
    for part in range(3):
        rows = slice(part * WIDTH, (part + 1) * WIDTH)
        weights_out[(part + 1) * WIDTH : (part + 2) * WIDTH, :] += dot_rows(
            low_full[...], grads[rows, :]
        )
    if first_layer:

        @pl.when(step == last)
        def _():
            shares[0].begin()
            for share in shares[1:]:
                share.stages[0].drain()
                share.stages[1].finish()
            shares[0].stages[0].receive()
            shares[0].add()
            shares[0].stages[1].start()
            shares[0].stages[0].drain()
            shares[0].stages[1].finish()

    else:
        if start:
            pl.when(step == last)(rows_sent.finish)
        if closes:
            gradient_sums(step, sizes, columns_prev, back_out, rows_out, scratch)
        else:

            @pl.when(step == last)
            def _():
                made[0] = scratch[0][...]
                made[1] = scratch[1][...]


def fixed(shape):
    return pl.BlockSpec(shape, lambda step: (0,) * len(shape))


def blocked(array, first=0):
    return pl.BlockSpec((1,) + array.shape[1:], lambda step: (first + step, 0, 0))


def layer_of(array, layer):
    shape = (1,) + array.shape[1:]
    return pl.BlockSpec(shape, lambda step: (layer,) + (0,) * (len(shape) - 1))


def rows_of(lanes):
    return pl.BlockSpec((lanes, WIDTH), lambda step: (step, 0))


ANY = pl.BlockSpec(memory_space=pl.ANY)


def shaped(shape, dtype=F32):
    return jax.ShapeDtypeStruct(shape, dtype)


def call(
    body, blocks, ins, in_specs, outs, out_specs, scratch, flops, collective=None, aliases=None
):
    arrays = list(ins) + (list(outs) if isinstance(outs, tuple) else [outs])
    size = sum(math.prod(a.shape) * a.dtype.itemsize for a in arrays)
    return pl.pallas_call(
        body,
        grid=(blocks,),
        in_specs=in_specs,
        out_specs=out_specs,
        out_shape=outs,
        scratch_shapes=scratch,
        input_output_aliases=aliases or {},
        compiler_params=pltpu.CompilerParams(
            dimension_semantics=("arbitrary",),
            vmem_limit_bytes=VMEM_BYTES,
            collective_id=collective,
            has_side_effects=collective is not None,
        ),
        cost_estimate=pl.CostEstimate(flops=flops, bytes_accessed=size, transcendentals=0),
    )(*ins)


STAT_SCRATCH = [
    pltpu.VMEM((WIDTH, WIDTH), F32),
    pltpu.VMEM((WIDTH, WIDTH), F32),
    pltpu.VMEM((WIDTH, WIDTH), F32),
    pltpu.VMEM((8, WIDTH), F32),
]
FORWARD_SLOT = [
    pltpu.VMEM((2, WIDTH, SPREAD), BF16),
    pltpu.VMEM((PAIR, SPREAD), F32),
    pltpu.VMEM((PAIR, SPREAD), BF16),
]
BACKWARD_SLOT = [
    pltpu.VMEM((2, WIDTH, SPREAD), BF16),
    pltpu.VMEM((2, WIDTH, SPREAD), BF16),
    pltpu.VMEM((PAIR, SPREAD), F32),
    pltpu.VMEM((PAIR, SPREAD), F32),
    pltpu.VMEM((PAIR, SPREAD), BF16),
    pltpu.VMEM((PAIR, SPREAD), BF16),
    pltpu.VMEM((2, HEAD_DIM, SPREAD), F32),
]
SUM_SCRATCH = [pltpu.VMEM((WIDTH, WIDTH), F32), pltpu.VMEM((WIDTH, WIDTH), F32)]


def swap_scratch(sizes):
    devices = sizes[0] * sizes[1]
    return [
        pltpu.VMEM((devices, 8, WIDTH), F32),
        pltpu.SemaphoreType.DMA,
        pltpu.SemaphoreType.DMA,
    ]


def head_gradient(sizes, inner, parts, batch_cotangent):
    sources, part, _, width = parts[0].shape
    series, horizon = batch_cotangent.shape[1:]
    group = lax.axis_index("dp") // inner
    cotangent = batch_cotangent
    if cotangent.shape[0] != sources:
        cotangent = lax.dynamic_slice_in_dim(cotangent, group * sources, sources, 0)
    at_once = 4
    shape = shaped((horizon, part * width), BF16)
    return call(
        head_gradient_body,
        sources // at_once,
        (*parts, cotangent),
        [
            pl.BlockSpec((at_once,) + rows.shape[1:], lambda step: (step, 0, 0, 0))
            for rows in parts
        ]
        + [pl.BlockSpec((at_once, series, horizon), lambda step: (step, 0, 0))],
        shape,
        fixed(shape.shape),
        [pltpu.VMEM((part, width, horizon), F32)],
        2 * sources * series * part * width * horizon,
    )


def spread_head(sizes, inner, rows):
    gathered = lax.all_gather(rows, "dp", axis=0)
    outer = sizes[0] // inner
    if outer > 1:
        gathered = jnp.sum(gathered.reshape((outer, inner) + rows.shape).astype(F32), axis=0)
    return gathered


def finish_outputs(rows, summed, tiles, layers, hidden):
    inner, horizon, columns = rows.shape
    at_once = math.gcd(inner, 4)
    shapes = (
        shaped((horizon, inner * columns)),
        shaped((layers, 3, WIDTH, WIDTH)),
        shaped((layers, WIDTH, WIDTH)),
        shaped((layers, WIDTH, hidden)),
        shaped((layers, hidden, WIDTH)),
        shaped((layers, 2, WIDTH)),
        shaped((layers, 2, WIDTH)),
    )
    head, *others = call(
        functools.partial(widen_body, layers),
        inner // at_once,
        (rows, summed, *tiles),
        [
            pl.BlockSpec((at_once, horizon, columns), lambda step: (step, 0, 0)),
            fixed(summed.shape),
        ]
        + [fixed(tile.shape) for tile in tiles],
        shapes,
        (pl.BlockSpec((horizon, at_once * columns), lambda step: (0, step)),)
        + tuple(fixed(shape.shape) for shape in shapes[1:]),
        [],
        1,
    )
    return *others, head.T


def per_device(
    sizes,
    embedded_segments,
    history_durations,
    segment_seen_indicator,
    query_key_value_matrices,
    mixing_result_matrices,
    first_dense_matrices,
    second_dense_matrices,
    batchnorm_scales,
    batchnorm_offsets,
    readout_matrix,
    prediction_cotangent,
):
    series, patches, width = embedded_segments.shape
    layers = query_key_value_matrices.shape[0]
    hidden = first_dense_matrices.shape[2]
    block = math.gcd(series, 16)
    blocks = series // block
    lanes = block * patches
    tokens = series * patches
    positions = jnp.arange(patches, dtype=jnp.int32)
    first_valid = patches - ((history_durations - 16) // 8 + 2)
    valid = (positions[None, :] >= first_valid[:, None]) & (segment_seen_indicator > 0)
    valid_rows = valid.astype(F32).reshape(blocks, 1, lanes)
    embedded = embedded_segments.reshape(tokens, width)
    horizon = readout_matrix.shape[1]
    readout_own = readout_matrix.T
    inner = math.gcd(sizes[0], patches // sizes[1])
    wide_f32 = shaped((blocks, width, lanes))
    columns_shape = shaped((6, WIDTH, WIDTH))
    back_shape = shaped((2, WIDTH, WIDTH))
    tile_shape = shaped((8, WIDTH))
    norm_specs = [fixed(batchnorm_scales.shape), fixed(batchnorm_offsets.shape)]
    half_rows = readout_matrix.shape[0]
    flat_spec, own_spec, other_spec = head_specs(horizon, half_rows, patches, series)
    pm_f32 = shaped((patches, series, width))
    pm_bf16 = shaped((patches, series, width), BF16)
    series_spec = pl.BlockSpec((patches, block, width), lambda step: (0, step, 0))
    weights_shape = shaped((4 * width, width))
    swap = swap_scratch(sizes)
    kept = []
    columns = None
    state = embedded
    batch_cotangent = lax.all_gather(prediction_cotangent, ("dp", "patch"), axis=0)
    for layer in range(layers):
        first = layer == 0
        qkv_shape = shaped((blocks, 3 * width, lanes), BF16)
        o_shape = shaped((blocks, width, lanes), BF16)
        lse_shape = shaped((blocks, block, SPREAD))
        ins = (state, readout_own) if first else (state, columns)
        specs = [rows_of(lanes), ANY] if first else [blocked(state), fixed(columns.shape)]
        makes_head = layer == layers - 1
        attended, qkv, mixed, lse, columns_one, *extra = call(
            functools.partial(attention_forward_body, sizes, layer, first, makes_head),
            blocks,
            ins
            + (
                query_key_value_matrices,
                mixing_result_matrices,
                valid_rows,
                batchnorm_scales,
                batchnorm_offsets,
            )
            + ((prediction_cotangent, readout_own, readout_other) if makes_head else ()),
            specs
            + [layer_of(query_key_value_matrices, layer), layer_of(mixing_result_matrices, layer)]
            + [blocked(valid_rows)]
            + norm_specs
            + (
                [fixed(prediction_cotangent.shape), own_spec, other_spec] if makes_head else []
            ),
            (wide_f32, qkv_shape, o_shape, lse_shape, columns_shape)
            + ((shaped(readout_own.shape, BF16),) if first else ())
            + ((pm_f32,) if makes_head else ()),
            (
                blocked(wide_f32),
                blocked(qkv_shape),
                blocked(o_shape),
                blocked(lse_shape),
                fixed(columns_shape.shape),
            )
            + ((ANY,) if first else ())
            + ((flat_spec,) if makes_head else ()),
            FORWARD_SLOT * 2
            + [
                pltpu.VMEM((width, lanes), F32),
                pltpu.VMEM((width, lanes), F32),
                pltpu.VMEM((lanes, width), BF16),
                pltpu.VMEM((block, SPREAD), F32),
                pltpu.VMEM((block, SPREAD), F32),
                pltpu.VMEM((3 * width, width), BF16),
                pltpu.VMEM((width, width), BF16),
            ]
            + STAT_SCRATCH
            + swap
            + ([pltpu.SemaphoreType.DMA((2,))] if first else []),
            20 * 10**9,
            2 * layer,
        )
        if first:
            readout_other, *extra = extra
        if makes_head:
            (grad_rows,) = extra
        summed, columns_two = call(
            functools.partial(feed_forward_body, sizes, layer),
            blocks,
            (
                attended,
                columns_one,
                first_dense_matrices,
                second_dense_matrices,
                valid_rows,
                batchnorm_scales,
                batchnorm_offsets,
            ),
            [
                blocked(attended),
                fixed(columns_one.shape),
                layer_of(first_dense_matrices, layer),
                layer_of(second_dense_matrices, layer),
                blocked(valid_rows),
            ]
            + norm_specs,
            (wide_f32, columns_shape),
            (blocked(wide_f32), fixed(columns_shape.shape)),
            [pltpu.VMEM((hidden, width), BF16), pltpu.VMEM((width, hidden), BF16)]
            + STAT_SCRATCH
            + swap,
            10 * 10**9,
            2 * layer + 1,
        )
        kept.append(
            (state, columns, attended, qkv, mixed, lse, columns_one, summed, columns_two)
        )
        state, columns = summed, columns_two

    sources = inner * sizes[1]
    own_patches = patches // sources
    early = max(5 * blocks // 9, 1)
    early_shape, late_shape = [
        shaped((sources, own_patches, count, width), BF16)
        for count in (early * block, series - early * block)
    ]
    flat, grad_state, back_two, rows_two = call(
        functools.partial(turn_body, sizes),
        blocks,
        (state, columns, valid_rows, grad_rows),
        [blocked(state), fixed(columns.shape), blocked(valid_rows), series_spec],
        (pm_bf16, wide_f32, back_shape, tile_shape),
        (series_spec, blocked(wide_f32), fixed(back_shape.shape), fixed(tile_shape.shape)),
        [pltpu.VMEM((lanes, width), F32)] + SUM_SCRATCH + swap,
        10**9,
        2 * layers,
    )
    out_shape = shaped((series, horizon), BF16)
    row_sems = [pltpu.SemaphoreType.DMA((2,))]

    weights, tiles = [], []
    for layer in reversed(range(layers)):
        first = layer == 0
        state, columns, attended, qkv, mixed, lse, columns_one, summed, columns_two = kept[layer]
        ships = layer == layers - 1
        grad_normed, feed_weights, back_one, rows_one, *extra = call(
            functools.partial(feed_backward_body, sizes, inner, ships),
            blocks,
            (
                grad_state,
                summed,
                attended,
                columns_two,
                back_two,
                columns_one,
                second_dense_matrices,
                first_dense_matrices,
                valid_rows,
            )
            + ((flat, readout_own, readout_other, flat) if ships else ()),
            [
                blocked(grad_state),
                blocked(summed),
                blocked(attended),
                fixed(columns_two.shape),
                fixed(back_two.shape),
                fixed(columns_one.shape),
                layer_of(second_dense_matrices, layer),
                layer_of(first_dense_matrices, layer),
                blocked(valid_rows),
            ]
            + ([flat_spec, own_spec, other_spec, ANY] if ships else []),
            (wide_f32, weights_shape, back_shape, tile_shape)
            + ((out_shape, early_shape) if ships else ()),
            (
                blocked(wide_f32),
                fixed(weights_shape.shape),
                fixed(back_shape.shape),
                fixed(tile_shape.shape),
            )
            + ((fixed(out_shape.shape), ANY) if ships else ()),
            ([pltpu.VMEM(out_shape.shape, F32)] if ships else [])
            + [
                pltpu.VMEM((hidden, lanes), BF16),
                pltpu.VMEM((width, lanes), BF16),
                pltpu.VMEM((width, lanes), BF16),
                pltpu.VMEM((hidden, lanes), BF16),
                pltpu.VMEM((hidden, width), BF16),
            ]
            + SUM_SCRATCH
            + swap
            + (row_sems if ships else []),
            20 * 10**9,
            2 * layers + 1 + 2 * layer,
        )
        if ships:
            predictions, early_rows = extra
        tiles = [rows_one, rows_two] + tiles
        scratch = BACKWARD_SLOT * 2 + [
            pltpu.VMEM((width, lanes), BF16),
            pltpu.VMEM((width, lanes), F32),
            pltpu.VMEM((width, lanes), F32),
            pltpu.VMEM((lanes, width), BF16),
            pltpu.VMEM((lanes, width), BF16),
            pltpu.VMEM((3 * width, lanes), BF16),
            pltpu.VMEM((width, 3 * width), BF16),
        ]
        ins = (
            grad_normed,
            attended,
            qkv,
            mixed,
            lse,
            valid_rows,
            columns_one,
            back_one,
            mixing_result_matrices,
            query_key_value_matrices,
            state,
        )

        def specs_from(at):
            return [
                blocked(grad_normed, at),
                blocked(attended, at),
                blocked(qkv, at),
                blocked(mixed, at),
                blocked(lse, at),
                blocked(valid_rows, at),
                fixed(columns_one.shape),
                fixed(back_one.shape),
                layer_of(mixing_result_matrices, layer),
                layer_of(query_key_value_matrices, layer),
            ]

        if first:
            others = tuple(weights) + (feed_weights,)
            devices = inner * sizes[1]
            summed_shape = shaped(
                (1 + len(others),) + weights_shape.shape, sharing_dtype(devices)
            )
            input_grad, summed_weights = call(
                functools.partial(attention_backward_body, sizes, inner, True, True, True, 0),
                blocks,
                ins + others,
                specs_from(0) + [rows_of(lanes)] + [fixed(weights_shape.shape)] * len(others),
                (shaped((tokens, width), BF16), summed_shape),
                (rows_of(lanes), ANY),
                scratch
                + [pltpu.VMEM(weights_shape.shape, F32)]
                + sharing_scratch(devices) * (1 + len(others)),
                50 * 10**9,
                2 * layers + 2 + 2 * layer,
            )
        else:
            start = early * block if ships and early < blocks else 0
            cut = (blocks + 1) // 2 if start else 0
            carried = ()
            if start:
                grad_state, attention_weights, sums, late_rows = call(
                    functools.partial(
                        attention_backward_body, sizes, inner, False, True, False, start
                    ),
                    cut,
                    ins + (columns, flat),
                    specs_from(0) + [blocked(state), fixed(columns.shape), ANY],
                    (wide_f32, weights_shape, back_shape, late_shape),
                    (
                        blocked(wide_f32),
                        fixed(weights_shape.shape),
                        fixed(back_shape.shape),
                        ANY,
                    ),
                    scratch + SUM_SCRATCH + swap + row_sems,
                    25 * 10**9,
                    4 * layers + 1,
                )
                carried = (grad_state, attention_weights, sums)
                parts = (early_rows, late_rows)
            elif ships:
                parts = (early_rows,)
            if ships:
                head_rows = head_gradient(sizes, inner, parts, batch_cotangent)
                (*carried, grad_normed), head_rows = lax.optimization_barrier(
                    ((*carried, grad_normed), head_rows)
                )
                head_rows = spread_head(sizes, inner, head_rows)
            grad_state, attention_weights, back_two, rows_two = call(
                functools.partial(
                    attention_backward_body, sizes, inner, False, not carried, True, 0
                ),
                blocks - cut,
                (grad_normed,) + ins[1:] + (columns, *carried),
                specs_from(cut)
                + [blocked(state, cut), fixed(columns.shape)]
                + (
                    [ANY, fixed(weights_shape.shape), fixed(back_shape.shape)]
                    if carried
                    else []
                ),
                (wide_f32, weights_shape, back_shape, tile_shape),
                (
                    blocked(wide_f32, cut),
                    fixed(weights_shape.shape),
                    fixed(back_shape.shape),
                    fixed(tile_shape.shape),
                ),
                scratch + SUM_SCRATCH + swap,
                25 * 10**9,
                2 * layers + 2 + 2 * layer,
                {len(ins) + 1: 0} if carried else None,
            )
            weights += [feed_weights, attention_weights]
    if devices < sizes[0] * sizes[1]:
        summed_weights = lax.psum(summed_weights.astype(F32), ("dp", "patch")) / devices
    return (
        predictions,
        input_grad.reshape(series, patches, width),
        *finish_outputs(head_rows, summed_weights, tiles, layers, hidden),
    )


def solution(mesh):
    placed = (
        P(("dp", "patch"), None, None),
        P(("dp", "patch")),
        P(("dp", "patch"), None),
        P(),
        P(),
        P(),
        P(),
        P(),
        P(),
        P("patch", None),
        P(("dp", "patch"), None),
    )
    sizes = (mesh.shape["dp"], mesh.shape["patch"])
    return jax.shard_map(
        functools.partial(per_device, sizes),
        mesh=mesh,
        in_specs=placed,
        out_specs=(
            P(("dp", "patch"), None),
            P(("dp", "patch"), None, None),
            P(),
            P(),
            P(),
            P(),
            P(),
            P(),
            P("patch", None),
        ),
        check_vma=False,
    )
```

```python
import functools
import math

import jax
import jax.numpy as jnp
from jax import lax
from jax.experimental import pallas as pl
from jax.experimental.pallas import tpu as pltpu
from jax.sharding import PartitionSpec as P

HEADS = 16
HEAD_DIM = 8
WIDTH = 128
PATCHES = 64
PAIR = 2 * PATCHES
GROUPS = 4
GROUP_ROWS = WIDTH // GROUPS
GROUP_LANES = HEADS // GROUPS * PATCHES
SPREAD = HEADS * PATCHES
EPS = 1e-05
MASKED = -1e30
SCALE = HEAD_DIM**-0.5
SCALE_LOG2 = SCALE * math.log2(math.e)
GELU_IN = math.sqrt(2.0 / math.pi)
GELU_CUBE = 0.044715
CHUNK = 1024
READOUT_CHUNKS = 4
F32 = jnp.float32
BF16 = jnp.bfloat16
VMEM_BYTES = 60 * 2**20


def dot(left, right):
    return lax.dot_general(left, right, (((1,), (0,)), ((), ())), preferred_element_type=F32)


def dot_rows(left, right):
    return lax.dot_general(left, right, (((1,), (1,)), ((), ())), preferred_element_type=F32)


def at_layer(ref, layer):
    return ref.at[pl.ds(layer, 1)]


def turn(matrix):
    return matrix.astype(F32).T.astype(matrix.dtype)


def wide(column, lanes):
    return jnp.concatenate([column] * (lanes // WIDTH), axis=1)


def fold_lanes(values):
    total = values[:, :WIDTH]
    for start in range(WIDTH, values.shape[1], WIDTH):
        total = total + values[:, start : start + WIDTH]
    return total


def fold_heads(values):
    return jnp.concatenate([values] * (GROUP_LANES // WIDTH), axis=1)


def side_masks():
    lane = lax.broadcasted_iota(jnp.int32, (WIDTH, PAIR), 1)
    row = lax.broadcasted_iota(jnp.int32, (WIDTH, PAIR), 0)
    left = lane < PATCHES
    even = (row // HEAD_DIM) % 2 == 0
    return left, even


def token_mask(valid):
    return jnp.broadcast_to(valid, (WIDTH, valid.shape[1])).T


def shown_keys(keys, mask):
    parts = []
    for start in range(0, keys.shape[0], PATCHES):
        own = keys[start : start + PATCHES]
        parts.append(jnp.where(mask[start : start + PATCHES] > 0.5, own, own[PATCHES - 1 :]))
    return jnp.concatenate(parts, axis=0)


def spread_pair(tile, left, even, target):
    turned = pltpu.roll(tile, PATCHES, 1)
    keep = left == even
    first = jnp.where(keep, jnp.where(even, tile, turned), 0.0).astype(BF16)
    second = jnp.where(keep, jnp.where(even, turned, tile), 0.0).astype(BF16)
    step = 2 * HEAD_DIM
    for index in range(HEADS // 2):
        rows = slice(index * step, (index + 1) * step)
        lanes = slice(index * PAIR, (index + 1) * PAIR)
        target[0, rows, lanes] = first[rows]
        target[1, rows, lanes] = second[rows]


def halves(tile, left):
    return (
        jnp.where(left, tile, 0.0).astype(BF16),
        jnp.where(left, 0.0, tile).astype(BF16),
    )


def gather_heads(first, second, left):
    parts = []
    for head in range(HEADS // GROUPS):
        rows = slice(head * HEAD_DIM, (head + 1) * HEAD_DIM)
        lanes = slice(head // 2 * PAIR, (head // 2 + 1) * PAIR)
        one, two = first[rows, lanes], second[rows, lanes]
        if head % 2 == 0:
            two = pltpu.roll(two, PATCHES, 1)
        else:
            one = pltpu.roll(one, PATCHES, 1)
        parts.append(jnp.where(left[:HEAD_DIM], one, two))
    return jnp.concatenate(parts, axis=0)


def pair_lanes(pair):
    start = pair * PAIR
    return pl.ds(start if isinstance(start, int) else pl.multiple_of(start, PAIR), PAIR)


def pipeline(pairs, slots, score, soften, mix):
    even, odd = slots
    score(0, even)

    def two_pairs(index, carry):
        first = 2 * index
        mix(jnp.maximum(first - 1, 0), odd)
        score(first + 1, odd)
        soften(first, even)
        mix(first, even)
        score(jnp.minimum(first + 2, pairs - 1), even)
        soften(first + 1, odd)
        return carry

    lax.fori_loop(0, pairs // 2, two_pairs, 0, unroll=True)
    mix(pairs - 1, odd)


def chunks(lanes, work):
    for start in range(0, lanes, CHUNK):
        work(slice(start, start + CHUNK))


def device_at(index, sizes):
    return index // sizes[1], lax.rem(index, sizes[1])


def greet(step, sizes):
    others = sizes[0] * sizes[1]
    own = lax.axis_index("dp") * sizes[1] + lax.axis_index("patch")
    barrier = pltpu.get_barrier_semaphore()

    @pl.when(step == 0)
    def _():
        def signal(offset, carry):
            target = device_at(lax.rem(own + offset, others), sizes)
            pl.semaphore_signal(
                barrier, inc=1, device_id=target, device_id_type=pl.DeviceIdType.MESH
            )
            return carry

        lax.fori_loop(1, others, signal, 0)


def met(sizes):
    pl.semaphore_wait(pltpu.get_barrier_semaphore(), sizes[0] * sizes[1] - 1)


def second_step():
    return jnp.minimum(1, pl.num_programs(0) - 1)


def swap_tiles(sizes, tiles, send, arrive):
    others = sizes[0] * sizes[1]
    own = lax.axis_index("dp") * sizes[1] + lax.axis_index("patch")

    def start(offset, carry):
        pltpu.make_async_remote_copy(
            src_ref=tiles.at[own],
            dst_ref=tiles.at[own],
            send_sem=send,
            recv_sem=arrive,
            device_id=device_at(lax.rem(own + offset, others), sizes),
            device_id_type=pl.DeviceIdType.MESH,
        ).start()
        return carry

    lax.fori_loop(1, others, start, 0)
    await_bytes(tiles.at[pl.ds(0, others - 1)], arrive)
    await_bytes(tiles.at[pl.ds(0, others - 1)], send)


def await_bytes(like, sem):
    pltpu.make_async_copy(like, like, sem).wait()


def readout_copy(source, target, sems):
    return pltpu.make_async_remote_copy(
        src_ref=source,
        dst_ref=target,
        send_sem=sems.at[0],
        recv_sem=sems.at[1],
        device_id=(lax.axis_index("dp"), 1 - lax.axis_index("patch")),
        device_id_type=pl.DeviceIdType.MESH,
    )


def own_part(sizes, inner):
    chip = lax.axis_index("dp")
    return chip // inner, lax.rem(chip, inner) * sizes[1] + lax.axis_index("patch")


def first_patch(sizes, inner, patches, place):
    half = lax.rem(place + lax.axis_index("patch"), sizes[1])
    return (half * inner + place // sizes[1]) * (patches // (inner * sizes[1]))


class Spread:
    def __init__(self, sizes, inner, source, target, like, send, arrive, pieces=1):
        self.sizes, self.inner, self.pieces = sizes, inner, pieces
        self.source, self.target, self.like = source, target, like
        self.send, self.arrive = send, arrive
        self.devices = inner * sizes[1]
        self.group, self.own = own_part(sizes, inner)

    def start(self):
        def piece(ref, index):
            size = ref.shape[0] // self.pieces
            return ref if self.pieces == 1 else ref.at[pl.ds(index * size, size)]

        def begin(count, carry):
            index = (count - 1) // (self.devices - 1)
            offset = count - index * (self.devices - 1)
            other = lax.rem(self.own + offset, self.devices)
            pltpu.make_async_remote_copy(
                src_ref=piece(self.source(other), index),
                dst_ref=piece(self.target(self.own), index),
                send_sem=self.send,
                recv_sem=self.arrive,
                device_id=(
                    self.group * self.inner + other // self.sizes[1],
                    lax.rem(other, self.sizes[1]),
                ),
                device_id_type=pl.DeviceIdType.MESH,
            ).start()
            return carry

        pltpu.make_async_copy(
            self.source(self.own), self.target(self.own), self.arrive
        ).start()
        lax.fori_loop(1, self.pieces * (self.devices - 1) + 1, begin, 0)

    def receive(self):
        await_bytes(self.like(self.devices), self.arrive)

    def drain(self):
        await_bytes(self.like(self.devices - 1), self.send)

    def finish(self):
        self.receive()
        self.drain()


class Sharing:
    def __init__(self, sizes, inner, whole, source, slots, share, target, sems):
        rows = slots.shape[1]
        self.whole, self.source, self.slots, self.share = whole, source, slots, share

        def part(ref, place):
            return ref.at[pl.ds(pl.multiple_of(place * rows, rows), rows)]

        self.stages = [
            Spread(
                sizes,
                inner,
                lambda place: part(source, place),
                lambda place: slots.at[place],
                lambda count: slots.at[pl.ds(0, count)],
                sems.at[0, 0],
                sems.at[0, 1],
            ),
            Spread(
                sizes,
                inner,
                lambda place: share,
                lambda place: part(target, place),
                lambda count: target.at[pl.ds(0, rows * count)],
                sems.at[1, 0],
                sems.at[1, 1],
            ),
        ]

    def begin(self):
        self.source[...] = self.whole[...].astype(self.source.dtype)
        self.stages[0].start()

    def add(self):
        total = self.slots[0].astype(F32)
        for place in range(1, self.slots.shape[0]):
            total = total + self.slots[place].astype(F32)
        self.share[...] = total.astype(self.share.dtype)


def sharing_dtype(devices):
    return BF16 if 4 * WIDTH // devices % 16 == 0 else F32


def sharing_scratch(devices):
    rows = 4 * WIDTH // devices
    dtype = sharing_dtype(devices)
    return [
        pltpu.VMEM((4 * WIDTH, WIDTH), dtype),
        pltpu.VMEM((devices, rows, WIDTH), dtype),
        pltpu.VMEM((rows, WIDTH), dtype),
        pltpu.SemaphoreType.DMA((2, 2)),
    ]


def ship_rows(sizes, inner, flat, start, slots, send, arrive):
    patches = flat.shape[0]
    part, count = slots.shape[1:3]
    return Spread(
        sizes,
        inner,
        lambda place: flat.at[
            pl.ds(first_patch(sizes, inner, patches, place), part), pl.ds(start, count)
        ],
        lambda slot: slots.at[slot],
        lambda places: slots.at[pl.ds(0, places)],
        send,
        arrive,
        part,
    )


def partner_copy(sizes, inner, partial, got, sems):
    chip = lax.axis_index("dp")
    half = lax.rem(chip, inner) // (inner // 2)
    other = chip + (1 - 2 * half) * (inner // 2)
    return half, pltpu.make_async_remote_copy(
        src_ref=partial.at[1 - half],
        dst_ref=got,
        send_sem=sems.at[0],
        recv_sem=sems.at[1],
        device_id=(other, lax.axis_index("patch")),
        device_id_type=pl.DeviceIdType.MESH,
    )


def as_columns(row):
    return jnp.broadcast_to(row, (WIDTH, WIDTH)).T


def norm_stats(step, sizes, values, valid, gains, out, scratch):
    pivot, sums, squares, count, tiles, send, arrive = scratch
    lanes = valid.shape[-1]

    @pl.when(step == 0)
    def _():
        own = jnp.sum(valid[...])
        first = jnp.sum(fold_lanes(values[...] * valid[...]), axis=1, keepdims=True) / own
        pivot[...] = jnp.broadcast_to(first, (WIDTH, WIDTH))
        sums[...] = jnp.zeros_like(sums)
        squares[...] = jnp.zeros_like(squares)
        count[...] = jnp.zeros_like(count)

    def add(at):
        centred = (values[:, at] - wide(pivot[...], CHUNK)) * valid[:, at]
        sums[...] += fold_lanes(centred)
        squares[...] += fold_lanes(centred * centred)
        count[...] += jnp.broadcast_to(fold_lanes(valid[:, at]), count.shape)

    chunks(lanes, add)

    @pl.when(step == pl.num_programs(0) - 1)
    def _():
        own = lax.axis_index("dp") * sizes[1] + lax.axis_index("patch")
        total = jnp.broadcast_to(jnp.sum(count[0:1, :]), (1, WIDTH))
        shift = jnp.sum(sums[...].T, axis=0, keepdims=True)
        square = jnp.sum(squares[...].T, axis=0, keepdims=True)
        tiles[own, 0:1, :] = pivot[...].T[0:1, :] + shift / total
        tiles[own, 1:2, :] = square - shift * shift / total
        tiles[own, 2:3, :] = total
        tiles[own, 3:4, :] = total
        swap_tiles(sizes, tiles, send, arrive)
        means, spreads, counts = tiles[:, 0, :], tiles[:, 1, :], tiles[:, 2, :]
        total = jnp.sum(counts, axis=0, keepdims=True)
        mean = jnp.sum(means * counts, axis=0, keepdims=True) / total
        apart = means - mean
        variance = jnp.sum(spreads + counts * (apart * apart), axis=0, keepdims=True) / total
        inverse = lax.rsqrt(variance + EPS)
        out[0] = as_columns(mean)
        out[1] = as_columns(inverse)
        out[2] = as_columns(inverse * gains[0])
        out[3] = as_columns(gains[1])
        out[4] = as_columns(total)
        out[5] = as_columns(gains[0])


def add_gradient(grad, normal, valid, scratch):
    weighted = grad * valid
    scratch[0][...] += fold_lanes(weighted * normal)
    scratch[1][...] += fold_lanes(weighted)


def clear_gradient(step, scratch):
    @pl.when(step == 0)
    def _():
        scratch[0][...] = jnp.zeros_like(scratch[0])
        scratch[1][...] = jnp.zeros_like(scratch[1])


def gradient_sums(step, sizes, columns, columns_out, rows_out, scratch):
    by_normal, plain, tiles, send, arrive = scratch

    @pl.when(step == pl.num_programs(0) - 1)
    def _():
        own = lax.axis_index("dp") * sizes[1] + lax.axis_index("patch")
        tiles[own, 0:1, :] = jnp.sum(by_normal[...].T, axis=0, keepdims=True)
        tiles[own, 1:2, :] = jnp.sum(plain[...].T, axis=0, keepdims=True)
        swap_tiles(sizes, tiles, send, arrive)
        summed = jnp.sum(tiles[...], axis=0)
        rows_out[...] = summed
        total = columns[4]
        columns_out[0] = as_columns(summed[0:1, :]) / total
        columns_out[1] = as_columns(summed[1:2, :]) / total


def apply_norm(values, columns):
    lanes = values.shape[1]
    return (values - wide(columns[0], lanes)) * wide(columns[2], lanes) + wide(columns[3], lanes)


def normalise(values, columns):
    lanes = values.shape[1]
    return (values - wide(columns[0], lanes)) * wide(columns[1], lanes)


def back_norm(grad, normal, valid, columns, back_columns):
    lanes = grad.shape[1]
    inner = wide(back_columns[1], lanes) + normal * wide(back_columns[0], lanes)
    return wide(columns[2], lanes) * (grad - valid * inner)


def attention_forward_body(sizes, layer, first_layer, makes_head, *refs):
    if first_layer:
        x_ref, readout, refs = refs[0], refs[1], refs[2:]
        columns = None
    else:
        x_ref, columns, refs = refs[0], refs[1], refs[2:]
    w_in_ref, w_out_ref, valid_ref, scales, offsets = refs[:5]
    refs = refs[5:]
    if makes_head:
        head_refs, refs = refs[:3], refs[3:]
    h_out, qkv_out, o_out, lse_out, columns_out = refs[:5]
    refs = refs[5:]
    if first_layer:
        readout_out, readout_sems = refs[0], refs[-1]
        refs = refs[1:-1]
    if makes_head:
        head_refs, refs = head_refs + refs[:1], refs[1:]
    size = len(FORWARD_SLOT)
    slots, refs = (refs[:size], refs[size : 2 * size]), refs[2 * size :]
    (x_full, q_full, k_rows, tops, sums, w_in, w_out), scratch = refs[:7], refs[7:]
    w_in_ref, w_out_ref = at_layer(w_in_ref, layer), at_layer(w_out_ref, layer)
    step = pl.program_id(0)
    greet(step, sizes)

    @pl.when(step == second_step())
    def _():
        met(sizes)
        if first_layer:
            readout_copy(readout, readout_out, readout_sems).start()

    lanes = h_out.shape[-1]
    pairs = lanes // PAIR

    @pl.when(step == 0)
    def _():
        for slot in slots:
            slot[0][...] = jnp.zeros_like(slot[0])
        for part in range(3):
            w_in[part * WIDTH : (part + 1) * WIDTH, :] = turn(w_in_ref[0, part])
        w_out[...] = turn(w_out_ref[0])

    if makes_head:
        head_backward(step, *head_refs)

    def project(at):
        x = x_ref[at, :].astype(F32).T if first_layer else apply_norm(x_ref[0, :, at], columns)
        x_full[:, at] = x
        low = x.astype(BF16)
        q = dot(w_in[0:WIDTH, :], low)
        q_full[:, at] = q
        qkv_out[0, 0:WIDTH, at] = q.astype(BF16)
        k = dot(w_in[WIDTH : 2 * WIDTH, :], low)
        k_rows[at, :] = shown_keys(k.T, token_mask(valid_ref[0, :, at])).astype(BF16)
        qkv_out[0, WIDTH : 2 * WIDTH, at] = k.astype(BF16)
        qkv_out[0, 2 * WIDTH :, at] = dot(w_in[2 * WIDTH :, :], low).astype(BF16)

    chunks(lanes, project)
    left, even = side_masks()

    def score(pair, slot):
        spread, scores, _ = slot
        at = pair_lanes(pair)
        spread_pair(q_full[:, at], left, even, spread)
        keys = k_rows[at, :]
        for side in range(2):
            own = slice(side * PATCHES, (side + 1) * PATCHES)
            for group in range(GROUPS):
                cut = slice(group * GROUP_LANES, (group + 1) * GROUP_LANES)
                scores[own, cut] = dot(keys[own], spread[side, :, cut])

    def soften(pair, slot):
        _, scores, weights = slot
        for side in range(2):
            own = slice(side * PATCHES, (side + 1) * PATCHES)
            for group in range(GROUPS):
                cut = slice(group * GROUP_LANES, (group + 1) * GROUP_LANES)
                shown = scores[own, cut]
                top = jnp.max(shown, axis=0, keepdims=True)
                weights[own, cut] = jnp.exp2((shown - top) * SCALE_LOG2).astype(BF16)
                tops[pl.ds(2 * pair + side, 1), cut] = top

    def mix(pair, slot):
        _, _, weights = slot
        at = pair_lanes(pair)
        valid = valid_ref[0, :, at]
        v_one, v_two = halves(qkv_out[0, 2 * WIDTH :, at].astype(F32) * valid, left)
        ones = jnp.broadcast_to(valid, (HEAD_DIM, PAIR))
        some = left[:HEAD_DIM]
        ones = jnp.concatenate([jnp.where(some, ones, 0.0), jnp.where(some, 0.0, ones)], axis=0)
        ones = ones.astype(BF16)
        for group in range(GROUPS):
            cut = slice(group * GROUP_LANES, (group + 1) * GROUP_LANES)
            rows = slice(group * GROUP_ROWS, (group + 1) * GROUP_ROWS)
            mixed = dot(
                jnp.concatenate([v_one[rows], v_two[rows], ones], axis=0), weights[:, cut]
            )
            products = []
            for side in range(2):
                start = 2 * GROUP_ROWS + side * HEAD_DIM
                total = mixed[start : start + HEAD_DIM]
                sums[pl.ds(2 * pair + side, 1), cut] = total[0:1]
                inverse = jnp.concatenate([1.0 / total] * (GROUP_ROWS // HEAD_DIM), axis=0)
                products.append(mixed[side * GROUP_ROWS : (side + 1) * GROUP_ROWS] * inverse)
            o_out[0, rows, at] = gather_heads(*products, left).astype(BF16)

    pipeline(pairs, slots, score, soften, mix)
    lse_out[0] = tops[...] * SCALE_LOG2 + jnp.log2(sums[...])

    def attend(at):
        h_out[0, :, at] = x_full[:, at] + dot(w_out[...], o_out[0, :, at])

    chunks(lanes, attend)
    if first_layer:

        @pl.when(step == pl.num_programs(0) - 1)
        def _():
            readout_copy(readout, readout_out, readout_sems).wait()

    gains = scales[layer, 0:1, :], offsets[layer, 0:1, :]
    norm_stats(step, sizes, h_out.at[0], valid_ref.at[0], gains, columns_out, scratch)


def feed_forward_body(
    sizes, layer, h_ref, columns, w_up_ref, w_down_ref, valid_ref, scales, offsets,
    f_out, columns_out, w_up, w_down, *scratch,
):
    w_up_ref, w_down_ref = at_layer(w_up_ref, layer), at_layer(w_down_ref, layer)
    step = pl.program_id(0)
    greet(step, sizes)

    @pl.when(step == second_step())
    def _():
        met(sizes)

    @pl.when(step == 0)
    def _():
        w_up[...] = turn(w_up_ref[0])
        w_down[...] = turn(w_down_ref[0])

    def feed(at):
        normed = apply_norm(h_ref[0, :, at], columns)
        low = normed.astype(BF16)
        active = []
        for start in range(0, w_up.shape[0], WIDTH):
            u = dot(w_up[start : start + WIDTH, :], low).astype(BF16).astype(F32)
            bent = jnp.tanh(u * (GELU_IN + (GELU_IN * GELU_CUBE) * (u * u)))
            half = 0.5 * u
            active.append((half + half * bent).astype(BF16))
        f_out[0, :, at] = normed + dot(w_down[...], jnp.concatenate(active, axis=0))

    chunks(h_ref.shape[-1], feed)
    gains = scales[layer, 1:2, :], offsets[layer, 1:2, :]
    norm_stats(step, sizes, f_out.at[0], valid_ref.at[0], gains, columns_out, scratch)


def turn_body(
    sizes, inner, f_ref, columns, valid_ref, gz_ref, flat_out, gx_out, back_out, rows_out,
    slots_out, turned, sent, row_sems, *scratch,
):
    step = pl.program_id(0)
    patches, block = gz_ref.shape[:2]
    part = slots_out.shape[1]
    early = sent.shape[0]
    greet(step, sizes)

    def shipment(index):
        return Spread(
            sizes,
            inner // 2,
            lambda place: sent.at[
                index, pl.ds(first_patch(sizes, inner // 2, patches, place), part)
            ],
            lambda slot: slots_out.at[
                slot, :, pl.ds(pl.multiple_of(index * block, block), block)
            ],
            lambda places: slots_out.at[pl.ds(0, places), :, pl.ds(0, block)],
            row_sems.at[0, index],
            row_sems.at[1, index],
        )

    @pl.when(step == second_step())
    def _():
        met(sizes)

    @pl.when((step >= 1) & (step <= early))
    def _():
        shipment(step - 1).start()

    clear_gradient(step, scratch)
    shift = lax.axis_index("patch") * (patches // sizes[1])

    def rows_at(patch):
        return pl.ds(lax.rem(patch + shift, patches), block, stride=patches)

    def show(at):
        turned[at, :] = (apply_norm(f_ref[0, :, at], columns) * valid_ref[0, :, at]).T

    def take(at):
        valid = valid_ref[0, :, at]
        grad = turned[at, :].T * valid
        gx_out[0, :, at] = grad
        add_gradient(grad, normalise(f_ref[0, :, at], columns), valid, scratch)

    chunks(f_ref.shape[-1], show)
    for patch in range(patches):
        flat_out[patch] = turned[rows_at(patch), :].astype(BF16)
    for patch in range(patches):
        turned[rows_at(patch), :] = gz_ref[patch]
    chunks(f_ref.shape[-1], take)

    @pl.when(step < early)
    def _():
        sent[step] = flat_out[...]

    @pl.when(step == pl.num_programs(0) - 1)
    def _():
        for index in range(early):
            shipment(index).finish()

    gradient_sums(step, sizes, columns, back_out, rows_out, scratch)


def head_backward(step, cotangent, readout_own, readout_other, out):
    def rows(readout):
        grad = dot(cotangent[...], readout[...])
        for patch in range(out.shape[0]):
            out[patch] = grad[:, patch * WIDTH : (patch + 1) * WIDTH]

    pl.when(step < READOUT_CHUNKS)(lambda: rows(readout_own))
    pl.when((step >= READOUT_CHUNKS) & (step < 2 * READOUT_CHUNKS))(lambda: rows(readout_other))


def head_forward(step, flat, readout_own, readout_other, out, total):
    @pl.when(step == 0)
    def _():
        total[...] = jnp.zeros_like(total)

    def rows(readout):
        for patch in range(0, flat.shape[0], 2):
            pair = jnp.concatenate([flat[patch], flat[patch + 1]], axis=1)
            total[...] += dot_rows(pair, readout[:, patch * WIDTH : (patch + 2) * WIDTH])

    pl.when(step < READOUT_CHUNKS)(lambda: rows(readout_own))
    pl.when((step >= READOUT_CHUNKS) & (step < 2 * READOUT_CHUNKS))(lambda: rows(readout_other))

    @pl.when(step == 2 * READOUT_CHUNKS - 1)
    def _():
        out[...] = total[...].astype(out.dtype)


def head_specs(horizon, half_rows, patches, series):
    chunk = half_rows // READOUT_CHUNKS
    last = 2 * READOUT_CHUNKS - 1
    flat_spec = pl.BlockSpec(
        (chunk // WIDTH, series, WIDTH), lambda step: (jnp.minimum(step, last), 0, 0)
    )
    own_spec = pl.BlockSpec(
        (horizon, chunk), lambda step: (0, jnp.minimum(step, READOUT_CHUNKS - 1))
    )
    other_spec = pl.BlockSpec(
        (horizon, chunk),
        lambda step: (0, jnp.clip(step - READOUT_CHUNKS, 0, READOUT_CHUNKS - 1)),
    )
    return flat_spec, own_spec, other_spec


def head_gradient_body(half, *refs):
    *parts, cotangent, out, total = refs
    step = pl.program_id(0)

    @pl.when(step == 0)
    def _():
        total[...] = jnp.zeros_like(total)

    sources, part, _, width = parts[0].shape
    start = 0
    for rows in parts:
        count = rows.shape[2]
        right = cotangent[:, start : start + count].reshape(sources * count, -1)
        start += count
        for patch in range(part):
            left = rows[:, patch].reshape(sources * count, width)
            total[patch] += lax.dot_general(
                left, right, (((0,), (0,)), ((), ())), preferred_element_type=F32
            )

    @pl.when(step == pl.num_programs(0) - 1)
    def _():
        for patch in range(part):
            index, place = divmod(patch, part // 2)
            lanes = slice(place * width, (place + 1) * width)
            out[index, :, lanes] = total[patch].T.astype(out.dtype)


def widen_body(layers, *refs):
    rows, summed, *tiles = refs[: 2 + 2 * layers]
    out, in_out, out_out, up_out, down_out, gain_out, shift_out = refs[2 + 2 * layers :]
    width = rows.shape[-1]
    for at in range(2 * rows.shape[1]):
        out[:, at * width : (at + 1) * width] = rows[at % 2, at // 2].astype(out.dtype)

    @pl.when(pl.program_id(0) == 0)
    def _():
        for layer in range(layers):
            attention = 2 * (layers - layer) if layer else 0
            feed = 2 * (layers - layer) - 1
            out_out[layer] = summed[attention, 0:WIDTH, :].astype(F32)
            for part in range(3):
                rows_of_part = slice((part + 1) * WIDTH, (part + 2) * WIDTH)
                in_out[layer, part] = summed[attention, rows_of_part, :].astype(F32)
            up_out[layer, :, :WIDTH] = summed[feed, :WIDTH, :].astype(F32)
            up_out[layer, :, WIDTH:] = summed[feed, WIDTH : 2 * WIDTH, :].astype(F32)
            down_out[layer] = summed[feed, 2 * WIDTH :, :].astype(F32)
            for norm in range(2):
                tile = tiles[2 * layer + norm]
                gain_out[layer, norm : norm + 1, :] = tile[0:1, :]
                shift_out[layer, norm : norm + 1, :] = tile[1:2, :]


def feed_backward_body(sizes, inner, layer, ships, *refs):
    (gx_ref, f_ref, h_ref, columns_two, back_two, columns_one, w_down, w_up,
     valid_ref), refs = refs[:9], refs[9:]
    w_down, w_up = at_layer(w_down, layer), at_layer(w_up, layer)
    if ships:
        flat_chunk, readout_own, readout_other, flat, *refs = refs
        gy_out, weights_out, back_out, rows_out, out, slots_out, total, *scratch = refs
        scratch, row_sems = scratch[:-1], scratch[-1]
        rows_sent = ship_rows(
            sizes,
            inner // 2,
            flat,
            flat.shape[1] - slots_out.shape[2],
            slots_out,
            row_sems.at[0],
            row_sems.at[1],
        )
    else:
        gy_out, weights_out, back_out, rows_out, *scratch = refs
    step = pl.program_id(0)
    greet(step, sizes)

    @pl.when(step == second_step())
    def _():
        met(sizes)
        if ships:
            rows_sent.start()

    if ships:
        head_forward(step, flat_chunk, readout_own, readout_other, out, total)
    active_full, low_full, normed_full, units_full, w_up_turned, *scratch = scratch
    clear_gradient(step, scratch)

    @pl.when(step == 0)
    def _():
        weights_out[...] = jnp.zeros_like(weights_out)
        w_up_turned[...] = turn(w_up[0])

    def feed(at):
        valid = valid_ref[0, :, at]
        normed = apply_norm(h_ref[0, :, at], columns_one).astype(BF16)
        normed_full[:, at] = normed
        normal = normalise(f_ref[0, :, at], columns_two)
        grad = back_norm(gx_ref[0, :, at], normal, valid, columns_two, back_two)
        low = grad.astype(BF16)
        low_full[:, at] = low
        grad_units = []
        for start in range(0, w_down.shape[1], WIDTH):
            rows = slice(start, start + WIDTH)
            u = dot(w_up_turned[rows, :], normed).astype(BF16).astype(F32)
            square = u * u
            bent = jnp.tanh(u * (GELU_IN + (GELU_IN * GELU_CUBE) * square))
            half = 0.5 + 0.5 * bent
            active_full[rows, at] = (u * half).astype(BF16)
            inner = (0.5 * GELU_IN) + (1.5 * GELU_IN * GELU_CUBE) * square
            slope = half + (u * inner) * (1.0 - bent * bent)
            grad_units.append((dot(w_down[0, rows, :], low) * slope).astype(BF16))
            units_full[rows, at] = grad_units[-1]
        normal = normalise(h_ref[0, :, at], columns_one)
        grad_normed = grad + dot(w_up[0], jnp.concatenate(grad_units, axis=0))
        gy_out[0, :, at] = grad_normed
        add_gradient(grad_normed, normal, valid, scratch)

    chunks(gx_ref.shape[-1], feed)
    weights_out[2 * WIDTH :, :] += dot_rows(active_full[...], low_full[...])
    by_up = dot_rows(normed_full[...], units_full[...])
    weights_out[0:WIDTH, :] += by_up[:, :WIDTH]
    weights_out[WIDTH : 2 * WIDTH, :] += by_up[:, WIDTH:]
    if ships:
        pl.when(step == pl.num_programs(0) - 1)(rows_sent.finish)
    gradient_sums(step, sizes, columns_one, back_out, rows_out, scratch)


def attention_backward_body(sizes, inner, layer, opens, closes, start, *refs):
    first_layer = layer == 0
    (gy_ref, h_ref, qkv_ref, o_ref, lse_ref, valid_ref, columns_one, back_one, w_out, w_in_ref,
     x_ref), refs = refs[:11], refs[11:]
    w_out, w_in_ref = at_layer(w_out, layer), at_layer(w_in_ref, layer)
    taken = made = None
    if first_layer:
        ready, (gx_out, summed_out), refs = refs[:3], refs[3:5], refs[5:]
        arrays = 1 + len(ready)
        each = len(sharing_scratch(inner * sizes[1]))
        refs, weights_out, shared = (
            refs[: -1 - each * arrays],
            refs[-1 - each * arrays],
            refs[-each * arrays :],
        )
        shares = []
        for at, whole in enumerate((weights_out,) + tuple(ready)):
            source, slots, share, sems = shared[each * at : each * (at + 1)]
            shares.append(
                Sharing(sizes, inner, whole, source, slots, share, summed_out.at[at], sems)
            )
    else:
        columns_prev, *refs = refs
        if start:
            partial, *refs = refs
        if not opens:
            _, taken, *refs = refs
            taken, made = (taken, refs[0]), None
            refs = refs[1:]
        if closes:
            gx_out, weights_out, back_out, rows_out, *refs = refs
        else:
            gx_out, weights_out, made, *refs = refs
        if start:
            rows_out, *refs, got, row_sems = refs
            half, partner = partner_copy(sizes, inner, partial, got, row_sems)
        count = len(SUM_SCRATCH) + len(swap_scratch(sizes, 2))
        refs, scratch = refs[:-count], refs[-count:]
    size = len(BACKWARD_SLOT)
    slots = refs[:size], refs[size : 2 * size]
    low_full, grad_full, g_full, k_rows, v_rows, grads, w_in = refs[2 * size :]
    step = pl.program_id(0)
    last = pl.num_programs(0) - 1
    if closes or start:
        greet(step, sizes)

        @pl.when(step == second_step())
        def _():
            met(sizes)
            if first_layer:
                for share in shares[1:]:
                    share.begin()
            elif start:
                partner.start()

    if first_layer:

        @pl.when(step == jnp.maximum(second_step(), last // 2 + 1))
        def _():
            for share in shares[1:]:
                share.stages[0].receive()
                share.add()
                share.stages[1].start()

    lanes = valid_ref.shape[-1]
    pairs = lanes // PAIR

    @pl.when(step == 0)
    def _():
        for slot in slots:
            slot[0][...] = jnp.zeros_like(slot[0])
            slot[1][...] = jnp.zeros_like(slot[1])
        weights_out[...] = jnp.zeros_like(weights_out) if taken is None else taken[0][...]
        for part in range(3):
            w_in[:, part * WIDTH : (part + 1) * WIDTH] = w_in_ref[0, part]

    if not first_layer and taken is None:
        clear_gradient(step, scratch)
    elif not first_layer:

        @pl.when(step == 0)
        def _():
            scratch[0][...] = taken[1][0]
            scratch[1][...] = taken[1][1]

    def prepare(at):
        normal = normalise(h_ref[0, :, at], columns_one)
        grad = back_norm(gy_ref[0, :, at], normal, valid_ref[0, :, at], columns_one, back_one)
        grad_full[:, at] = grad
        low = grad.astype(BF16)
        low_full[:, at] = low
        g_full[:, at] = dot(w_out[0], low).astype(BF16).astype(F32)
        mask = token_mask(valid_ref[0, :, at])
        keys = shown_keys(qkv_ref[0, WIDTH : 2 * WIDTH, at].astype(F32).T, mask)
        k_rows[at, :] = keys.astype(BF16)
        v_rows[at, :] = (qkv_ref[0, 2 * WIDTH :, at].astype(F32).T * mask).astype(BF16)

    chunks(lanes, prepare)
    weights_out[0:WIDTH, :] += dot_rows(o_ref[0], low_full[...])
    left, even = side_masks()

    def score(pair, slot):
        spread_q, spread_g, scores, pulls, _, _, inner = slot
        at = pair_lanes(pair)
        spread_pair(qkv_ref[0, 0:WIDTH, at].astype(F32), left, even, spread_q)
        grad = g_full[:, at]
        spread_pair(grad, left, even, spread_g)
        keys = k_rows[at, :]
        content = v_rows[at, :]
        for side in range(2):
            own = slice(side * PATCHES, (side + 1) * PATCHES)
            for group in range(GROUPS):
                cut = slice(group * GROUP_LANES, (group + 1) * GROUP_LANES)
                scores[own, cut] = dot(keys[own], spread_q[side, :, cut])
                pulls[own, cut] = dot(content[own], spread_g[side, :, cut])
        products = grad * o_ref[0, :, at].astype(F32)
        some = left[:HEAD_DIM]
        for head in range(0, HEADS, 2):
            both = [
                jnp.broadcast_to(
                    jnp.sum(products[start : start + HEAD_DIM], axis=0, keepdims=True),
                    (HEAD_DIM, PAIR),
                )
                for start in (head * HEAD_DIM, (head + 1) * HEAD_DIM)
            ]
            turned = [pltpu.roll(row, PATCHES, 1) for row in both]
            lanes_of = slice(head * PATCHES, (head + 2) * PATCHES)
            inner[0, :, lanes_of] = jnp.where(some, both[0], turned[1])
            inner[1, :, lanes_of] = jnp.where(some, turned[0], both[1])

    def soften(pair, slot):
        _, _, scores, pulls, weights, slopes, inner = slot
        for side in range(2):
            own = slice(side * PATCHES, (side + 1) * PATCHES)
            for group in range(GROUPS):
                cut = slice(group * GROUP_LANES, (group + 1) * GROUP_LANES)
                total = lse_ref[0, pl.ds(2 * pair + side, 1), cut]
                weight = jnp.exp2(scores[own, cut] * SCALE_LOG2 - total)
                weights[own, cut] = weight.astype(BF16)
                mean = jnp.concatenate([inner[side, :, cut]] * (PATCHES // HEAD_DIM), axis=0)
                slopes[own, cut] = (weight * (pulls[own, cut] - mean)).astype(BF16)

    def mix(pair, slot):
        spread_q, spread_g, _, _, weights, slopes, _ = slot
        at = pair_lanes(pair)
        valid = valid_ref[0, :, at]
        k_one, k_two = halves(qkv_ref[0, WIDTH : 2 * WIDTH, at].astype(F32) * valid, left)
        own_left = left[:GROUP_ROWS]
        for group in range(GROUPS):
            cut = slice(group * GROUP_LANES, (group + 1) * GROUP_LANES)
            start = group * GROUP_ROWS
            rows = slice(start, start + GROUP_ROWS)
            weight = weights[:, cut]
            slope = slopes[:, cut]
            by_value = dot_rows(
                jnp.concatenate([spread_g[0, rows, cut], spread_g[1, rows, cut]], axis=0), weight
            )
            by_value = jnp.where(own_left, by_value[:GROUP_ROWS], by_value[GROUP_ROWS:])
            grads[2 * WIDTH + start : 2 * WIDTH + start + GROUP_ROWS, at] = (
                by_value * valid
            ).astype(BF16)
            by_key = dot_rows(
                jnp.concatenate([spread_q[0, rows, cut], spread_q[1, rows, cut]], axis=0), slope
            )
            by_key = jnp.where(own_left, by_key[:GROUP_ROWS], by_key[GROUP_ROWS:])
            grads[WIDTH + start : WIDTH + start + GROUP_ROWS, at] = (
                by_key * (valid * SCALE)
            ).astype(BF16)
            by_query = dot(jnp.concatenate([k_one[rows], k_two[rows]], axis=0), slope)
            grads[rows, at] = (
                gather_heads(by_query[:GROUP_ROWS], by_query[GROUP_ROWS:], left) * SCALE
            ).astype(BF16)

    pipeline(pairs, slots, score, soften, mix)

    def finish(at):
        if first_layer:
            low_full[:, at] = x_ref[at, :].astype(F32).T.astype(BF16)
        else:
            normal = normalise(x_ref[0, :, at], columns_prev)
            inputs = normal * wide(columns_prev[5], CHUNK) + wide(columns_prev[3], CHUNK)
            low_full[:, at] = inputs.astype(BF16)
        grad = grad_full[:, at] + dot(w_in[...], grads[:, at])
        if first_layer:
            gx_out[at, :] = grad.T.astype(BF16)
        else:
            gx_out[0, :, at] = grad
            add_gradient(grad, normal, valid_ref[0, :, at], scratch)

    chunks(lanes, finish)
    for part in range(3):
        rows = slice(part * WIDTH, (part + 1) * WIDTH)
        weights_out[(part + 1) * WIDTH : (part + 2) * WIDTH, :] += dot_rows(
            low_full[...], grads[rows, :]
        )
    if first_layer:

        @pl.when(step == last)
        def _():
            shares[0].begin()
            for share in shares[1:]:
                share.stages[0].drain()
                share.stages[1].finish()
            shares[0].stages[0].receive()
            shares[0].add()
            shares[0].stages[1].start()
            shares[0].stages[0].drain()
            shares[0].stages[1].finish()

    else:
        if start:

            @pl.when(step == last)
            def _():
                partner.wait()
                total = partial[half].astype(F32) + got[...].astype(F32)
                rows_out[...] = total.astype(rows_out.dtype)

        if closes:
            gradient_sums(step, sizes, columns_prev, back_out, rows_out, scratch)
        else:

            @pl.when(step == last)
            def _():
                made[0] = scratch[0][...]
                made[1] = scratch[1][...]


def fixed(shape):
    return pl.BlockSpec(memory_space=pltpu.VMEM)


def blocked(array, first=0):
    return pl.BlockSpec((1,) + array.shape[1:], lambda step: (first + step, 0, 0))


def rows_of(lanes):
    return pl.BlockSpec((lanes, WIDTH), lambda step: (step, 0))


ANY = pl.BlockSpec(memory_space=pl.ANY)


def shaped(shape, dtype=F32):
    return jax.ShapeDtypeStruct(shape, dtype)


def call(
    body, blocks, ins, in_specs, outs, out_specs, scratch, flops, collective=None, aliases=None
):
    arrays = list(ins) + (list(outs) if isinstance(outs, tuple) else [outs])
    size = sum(math.prod(a.shape) * a.dtype.itemsize for a in arrays)
    return pl.pallas_call(
        body,
        grid=(blocks,),
        in_specs=in_specs,
        out_specs=out_specs,
        out_shape=outs,
        scratch_shapes=scratch,
        input_output_aliases=aliases or {},
        compiler_params=pltpu.CompilerParams(
            dimension_semantics=("arbitrary",),
            vmem_limit_bytes=VMEM_BYTES,
            collective_id=collective,
            has_side_effects=collective is not None,
        ),
        cost_estimate=pl.CostEstimate(flops=flops, bytes_accessed=size, transcendentals=0),
    )(*ins)


STAT_SCRATCH = [
    pltpu.VMEM((WIDTH, WIDTH), F32),
    pltpu.VMEM((WIDTH, WIDTH), F32),
    pltpu.VMEM((WIDTH, WIDTH), F32),
    pltpu.VMEM((8, WIDTH), F32),
]
FORWARD_SLOT = [
    pltpu.VMEM((2, WIDTH, SPREAD), BF16),
    pltpu.VMEM((PAIR, SPREAD), F32),
    pltpu.VMEM((PAIR, SPREAD), BF16),
]
BACKWARD_SLOT = [
    pltpu.VMEM((2, WIDTH, SPREAD), BF16),
    pltpu.VMEM((2, WIDTH, SPREAD), BF16),
    pltpu.VMEM((PAIR, SPREAD), F32),
    pltpu.VMEM((PAIR, SPREAD), F32),
    pltpu.VMEM((PAIR, SPREAD), BF16),
    pltpu.VMEM((PAIR, SPREAD), BF16),
    pltpu.VMEM((2, HEAD_DIM, SPREAD), F32),
]
SUM_SCRATCH = [pltpu.VMEM((WIDTH, WIDTH), F32), pltpu.VMEM((WIDTH, WIDTH), F32)]


def swap_scratch(sizes, rows):
    devices = sizes[0] * sizes[1]
    return [
        pltpu.VMEM((devices, rows, WIDTH), F32),
        pltpu.SemaphoreType.DMA,
        pltpu.SemaphoreType.DMA,
    ]


def head_gradient(sizes, inner, parts, batch_cotangent):
    sources, part, _, width = parts[0].shape
    series, horizon = batch_cotangent.shape[1:]
    half = lax.axis_index("dp") // (inner // 2)
    at_once = 4
    steps = sources // at_once
    return pl.pallas_call(
        head_gradient_body,
        grid_spec=pltpu.PrefetchScalarGridSpec(
            num_scalar_prefetch=1,
            grid=(steps,),
            in_specs=[
                pl.BlockSpec((at_once,) + rows.shape[1:], lambda step, half: (step, 0, 0, 0))
                for rows in parts
            ]
            + [
                pl.BlockSpec(
                    (at_once, series, horizon), lambda step, half: (half[0] * steps + step, 0, 0)
                )
            ],
            out_specs=pl.BlockSpec(memory_space=pltpu.VMEM),
            scratch_shapes=[pltpu.VMEM((part, width, horizon), F32)],
        ),
        out_shape=shaped((2, horizon, part // 2 * width), BF16),
        compiler_params=pltpu.CompilerParams(
            dimension_semantics=("arbitrary",), vmem_limit_bytes=VMEM_BYTES
        ),
        cost_estimate=pl.CostEstimate(
            flops=2 * sources * series * part * width * horizon,
            bytes_accessed=2 * sources * series * (part * width + horizon),
            transcendentals=0,
        ),
    )(half.astype(jnp.int32).reshape(1), *parts, batch_cotangent)


def spread_head(sizes, inner, rows):
    gathered = lax.all_gather(rows, "dp", axis=0)
    outer = sizes[0] // inner
    if outer > 1:
        gathered = jnp.sum(gathered.reshape((outer, inner) + rows.shape).astype(F32), axis=0)
    return gathered


def finish_outputs(rows, summed, tiles, layers, hidden):
    inner, horizon, columns = rows.shape
    rows = rows.reshape(2, inner // 2, horizon, columns)
    at_once = math.gcd(inner, 4)
    shapes = (
        shaped((horizon, inner * columns)),
        shaped((layers, 3, WIDTH, WIDTH)),
        shaped((layers, WIDTH, WIDTH)),
        shaped((layers, WIDTH, hidden)),
        shaped((layers, hidden, WIDTH)),
        shaped((layers, 2, WIDTH)),
        shaped((layers, 2, WIDTH)),
    )
    head, *others = call(
        functools.partial(widen_body, layers),
        inner // at_once,
        (rows, summed, *tiles),
        [
            pl.BlockSpec((2, at_once // 2, horizon, columns), lambda step: (0, step, 0, 0)),
            fixed(summed.shape),
        ]
        + [fixed(tile.shape) for tile in tiles],
        shapes,
        (pl.BlockSpec((horizon, at_once * columns), lambda step: (0, step)),)
        + tuple(fixed(shape.shape) for shape in shapes[1:]),
        [],
        1,
    )
    return *others, head.T


def per_device(
    sizes,
    embedded_segments,
    history_durations,
    segment_seen_indicator,
    query_key_value_matrices,
    mixing_result_matrices,
    first_dense_matrices,
    second_dense_matrices,
    batchnorm_scales,
    batchnorm_offsets,
    readout_matrix,
    prediction_cotangent,
):
    series, patches, width = embedded_segments.shape
    layers = query_key_value_matrices.shape[0]
    hidden = first_dense_matrices.shape[2]
    block = math.gcd(series, 16)
    blocks = series // block
    lanes = block * patches
    tokens = series * patches
    positions = jnp.arange(patches, dtype=jnp.int32)
    first_valid = patches - ((history_durations - 16) // 8 + 2)
    valid = (positions[None, :] >= first_valid[:, None]) & (segment_seen_indicator > 0)
    valid_rows = valid.astype(F32).reshape(blocks, 1, lanes)
    embedded = embedded_segments.reshape(tokens, width)
    horizon = readout_matrix.shape[1]
    readout_own = readout_matrix.T
    inner = math.gcd(sizes[0], patches // sizes[1])
    wide_f32 = shaped((blocks, width, lanes))
    columns_shape = shaped((6, WIDTH, WIDTH))
    back_shape = shaped((2, WIDTH, WIDTH))
    tile_shape = shaped((2, WIDTH))
    norm_specs = [fixed(batchnorm_scales.shape), fixed(batchnorm_offsets.shape)]
    half_rows = readout_matrix.shape[0]
    flat_spec, own_spec, other_spec = head_specs(horizon, half_rows, patches, series)
    pm_f32 = shaped((patches, series, width))
    pm_bf16 = shaped((patches, series, width), BF16)
    series_spec = pl.BlockSpec((patches, block, width), lambda step: (0, step, 0))
    weights_shape = shaped((4 * width, width))
    stat_swap, sum_swap = swap_scratch(sizes, 4), swap_scratch(sizes, 2)
    kept = []
    columns = None
    state = embedded
    batch_cotangent = lax.all_gather(prediction_cotangent, ("dp", "patch"), axis=0)
    for layer in range(layers):
        first = layer == 0
        qkv_shape = shaped((blocks, 3 * width, lanes), BF16)
        o_shape = shaped((blocks, width, lanes), BF16)
        lse_shape = shaped((blocks, block, SPREAD))
        ins = (state, readout_own) if first else (state, columns)
        specs = [rows_of(lanes), ANY] if first else [blocked(state), fixed(columns.shape)]
        makes_head = layer == layers - 1
        attended, qkv, mixed, lse, columns_one, *extra = call(
            functools.partial(attention_forward_body, sizes, layer, first, makes_head),
            blocks,
            ins
            + (
                query_key_value_matrices,
                mixing_result_matrices,
                valid_rows,
                batchnorm_scales,
                batchnorm_offsets,
            )
            + ((prediction_cotangent, readout_own, readout_other) if makes_head else ()),
            specs
            + [fixed(query_key_value_matrices.shape), fixed(mixing_result_matrices.shape)]
            + [blocked(valid_rows)]
            + norm_specs
            + (
                [fixed(prediction_cotangent.shape), own_spec, other_spec] if makes_head else []
            ),
            (wide_f32, qkv_shape, o_shape, lse_shape, columns_shape)
            + ((shaped(readout_own.shape, BF16),) if first else ())
            + ((pm_f32,) if makes_head else ()),
            (
                blocked(wide_f32),
                blocked(qkv_shape),
                blocked(o_shape),
                blocked(lse_shape),
                fixed(columns_shape.shape),
            )
            + ((ANY,) if first else ())
            + ((flat_spec,) if makes_head else ()),
            FORWARD_SLOT * 2
            + [
                pltpu.VMEM((width, lanes), F32),
                pltpu.VMEM((width, lanes), F32),
                pltpu.VMEM((lanes, width), BF16),
                pltpu.VMEM((block, SPREAD), F32),
                pltpu.VMEM((block, SPREAD), F32),
                pltpu.VMEM((3 * width, width), BF16),
                pltpu.VMEM((width, width), BF16),
            ]
            + STAT_SCRATCH
            + stat_swap
            + ([pltpu.SemaphoreType.DMA((2,))] if first else []),
            20 * 10**9,
            2 * layer,
        )
        if first:
            readout_other, *extra = extra
        if makes_head:
            (grad_rows,) = extra
        summed, columns_two = call(
            functools.partial(feed_forward_body, sizes, layer),
            blocks,
            (
                attended,
                columns_one,
                first_dense_matrices,
                second_dense_matrices,
                valid_rows,
                batchnorm_scales,
                batchnorm_offsets,
            ),
            [
                blocked(attended),
                fixed(columns_one.shape),
                fixed(first_dense_matrices.shape),
                fixed(second_dense_matrices.shape),
                blocked(valid_rows),
            ]
            + norm_specs,
            (wide_f32, columns_shape),
            (blocked(wide_f32), fixed(columns_shape.shape)),
            [pltpu.VMEM((hidden, width), BF16), pltpu.VMEM((width, hidden), BF16)]
            + STAT_SCRATCH
            + stat_swap,
            10 * 10**9,
            2 * layer + 1,
        )
        kept.append(
            (state, columns, attended, qkv, mixed, lse, columns_one, summed, columns_two)
        )
        state, columns = summed, columns_two

    sources = inner // 2 * sizes[1]
    early = max(4 * blocks // 9, 1)
    early_shape, late_shape = [
        shaped((sources, patches // sources, count, width), BF16)
        for count in (early * block, series - early * block)
    ]
    rows_shape = shaped((horizon, patches // sources // 2 * width), BF16)
    flat, grad_state, back_two, rows_two, early_rows = call(
        functools.partial(turn_body, sizes, inner),
        blocks,
        (state, columns, valid_rows, grad_rows),
        [blocked(state), fixed(columns.shape), blocked(valid_rows), series_spec],
        (pm_bf16, wide_f32, back_shape, tile_shape, early_shape),
        (
            series_spec,
            blocked(wide_f32),
            fixed(back_shape.shape),
            fixed(tile_shape.shape),
            ANY,
        ),
        [
            pltpu.VMEM((lanes, width), F32),
            pltpu.VMEM((early, patches, block, width), BF16),
            pltpu.SemaphoreType.DMA((2, early)),
        ]
        + SUM_SCRATCH
        + sum_swap,
        10**9,
        2 * layers,
    )
    out_shape = shaped((series, horizon), BF16)
    row_sems = [pltpu.SemaphoreType.DMA((2,))]

    weights, tiles = [], []
    for layer in reversed(range(layers)):
        first = layer == 0
        state, columns, attended, qkv, mixed, lse, columns_one, summed, columns_two = kept[layer]
        ships = layer == layers - 1
        grad_normed, feed_weights, back_one, rows_one, *extra = call(
            functools.partial(feed_backward_body, sizes, inner, layer, ships),
            blocks,
            (
                grad_state,
                summed,
                attended,
                columns_two,
                back_two,
                columns_one,
                second_dense_matrices,
                first_dense_matrices,
                valid_rows,
            )
            + ((flat, readout_own, readout_other, flat) if ships else ()),
            [
                blocked(grad_state),
                blocked(summed),
                blocked(attended),
                fixed(columns_two.shape),
                fixed(back_two.shape),
                fixed(columns_one.shape),
                fixed(second_dense_matrices.shape),
                fixed(first_dense_matrices.shape),
                blocked(valid_rows),
            ]
            + ([flat_spec, own_spec, other_spec, ANY] if ships else []),
            (wide_f32, weights_shape, back_shape, tile_shape)
            + ((out_shape, late_shape) if ships else ()),
            (
                blocked(wide_f32),
                fixed(weights_shape.shape),
                fixed(back_shape.shape),
                fixed(tile_shape.shape),
            )
            + ((fixed(out_shape.shape), ANY) if ships else ()),
            ([pltpu.VMEM(out_shape.shape, F32)] if ships else [])
            + [
                pltpu.VMEM((hidden, lanes), BF16),
                pltpu.VMEM((width, lanes), BF16),
                pltpu.VMEM((width, lanes), BF16),
                pltpu.VMEM((hidden, lanes), BF16),
                pltpu.VMEM((hidden, width), BF16),
            ]
            + SUM_SCRATCH
            + sum_swap
            + (row_sems if ships else []),
            20 * 10**9,
            2 * layers + 1 + 2 * layer,
        )
        if ships:
            predictions, late_rows = extra
            partial = head_gradient(sizes, inner, (early_rows, late_rows), batch_cotangent)
            grad_normed, partial = lax.optimization_barrier((grad_normed, partial))
        tiles = [rows_one, rows_two] + tiles
        scratch = BACKWARD_SLOT * 2 + [
            pltpu.VMEM((width, lanes), BF16),
            pltpu.VMEM((width, lanes), F32),
            pltpu.VMEM((width, lanes), F32),
            pltpu.VMEM((lanes, width), BF16),
            pltpu.VMEM((lanes, width), BF16),
            pltpu.VMEM((3 * width, lanes), BF16),
            pltpu.VMEM((width, 3 * width), BF16),
        ]
        ins = (
            grad_normed,
            attended,
            qkv,
            mixed,
            lse,
            valid_rows,
            columns_one,
            back_one,
            mixing_result_matrices,
            query_key_value_matrices,
            state,
        )

        def specs_from(at):
            return [
                blocked(grad_normed, at),
                blocked(attended, at),
                blocked(qkv, at),
                blocked(mixed, at),
                blocked(lse, at),
                blocked(valid_rows, at),
                fixed(columns_one.shape),
                fixed(back_one.shape),
                fixed(mixing_result_matrices.shape),
                fixed(query_key_value_matrices.shape),
            ]

        if first:
            others = tuple(weights) + (feed_weights,)
            devices = inner * sizes[1]
            summed_shape = shaped(
                (1 + len(others),) + weights_shape.shape, sharing_dtype(devices)
            )
            input_grad, summed_weights = call(
                functools.partial(attention_backward_body, sizes, inner, layer, True, True, False),
                blocks,
                ins + others,
                specs_from(0) + [rows_of(lanes)] + [fixed(weights_shape.shape)] * len(others),
                (shaped((tokens, width), BF16), summed_shape),
                (rows_of(lanes), ANY),
                scratch
                + [pltpu.VMEM(weights_shape.shape, F32)]
                + sharing_scratch(devices) * (1 + len(others)),
                50 * 10**9,
                2 * layers + 2 + 2 * layer,
            )
        else:
            cut = (blocks + 1) // 2 if ships else 0
            carried = ()
            if ships:
                grad_state, attention_weights, sums, head_rows = call(
                    functools.partial(
                        attention_backward_body, sizes, inner, layer, True, False, True
                    ),
                    cut,
                    ins + (columns, partial),
                    specs_from(0)
                    + [blocked(state), fixed(columns.shape), fixed(partial.shape)],
                    (wide_f32, weights_shape, back_shape, rows_shape),
                    (
                        blocked(wide_f32),
                        fixed(weights_shape.shape),
                        fixed(back_shape.shape),
                        fixed(rows_shape.shape),
                    ),
                    scratch
                    + SUM_SCRATCH
                    + sum_swap
                    + [pltpu.VMEM(rows_shape.shape, BF16)]
                    + row_sems,
                    25 * 10**9,
                    4 * layers + 1,
                )
                (*carried, grad_normed), head_rows = lax.optimization_barrier(
                    ((grad_state, attention_weights, sums, grad_normed), head_rows)
                )
                head_rows = spread_head(sizes, inner, head_rows)
            grad_state, attention_weights, back_two, rows_two = call(
                functools.partial(
                    attention_backward_body, sizes, inner, layer, not carried, True, False
                ),
                blocks - cut,
                (grad_normed,) + ins[1:] + (columns, *carried),
                specs_from(cut)
                + [blocked(state, cut), fixed(columns.shape)]
                + (
                    [ANY, fixed(weights_shape.shape), fixed(back_shape.shape)]
                    if carried
                    else []
                ),
                (wide_f32, weights_shape, back_shape, tile_shape),
                (
                    blocked(wide_f32, cut),
                    fixed(weights_shape.shape),
                    fixed(back_shape.shape),
                    fixed(tile_shape.shape),
                ),
                scratch + SUM_SCRATCH + sum_swap,
                25 * 10**9,
                2 * layers + 2 + 2 * layer,
                {len(ins) + 1: 0} if carried else None,
            )
            weights += [feed_weights, attention_weights]
    if devices < sizes[0] * sizes[1]:
        summed_weights = lax.psum(summed_weights.astype(F32), ("dp", "patch")) / devices
    return (
        predictions,
        input_grad.reshape(series, patches, width),
        *finish_outputs(head_rows, summed_weights, tiles, layers, hidden),
    )


def solution(mesh):
    placed = (
        P(("dp", "patch"), None, None),
        P(("dp", "patch")),
        P(("dp", "patch"), None),
        P(),
        P(),
        P(),
        P(),
        P(),
        P(),
        P("patch", None),
        P(("dp", "patch"), None),
    )
    sizes = (mesh.shape["dp"], mesh.shape["patch"])
    return jax.shard_map(
        functools.partial(per_device, sizes),
        mesh=mesh,
        in_specs=placed,
        out_specs=(
            P(("dp", "patch"), None),
            P(("dp", "patch"), None, None),
            P(),
            P(),
            P(),
            P(),
            P(),
            P(),
            P("patch", None),
        ),
        check_vma=False,
    )
```

```python
import functools
import math

import jax
import jax.numpy as jnp
from jax import lax
from jax.experimental import pallas as pl
from jax.experimental.pallas import tpu as pltpu
from jax.sharding import PartitionSpec as P

HEADS = 16
HEAD_DIM = 8
WIDTH = 128
PATCHES = 64
PAIR = 2 * PATCHES
GROUPS = 4
GROUP_ROWS = WIDTH // GROUPS
GROUP_LANES = HEADS // GROUPS * PATCHES
SPREAD = HEADS * PATCHES
EPS = 1e-05
MASKED = -1e30
SCALE = HEAD_DIM**-0.5
SCALE_LOG2 = SCALE * math.log2(math.e)
GELU_IN = math.sqrt(2.0 / math.pi)
GELU_CUBE = 0.044715
CHUNK = 1024
READOUT_CHUNKS = 4
F32 = jnp.float32
BF16 = jnp.bfloat16
VMEM_BYTES = 60 * 2**20


def dot(left, right):
    return lax.dot_general(left, right, (((1,), (0,)), ((), ())), preferred_element_type=F32)


def dot_rows(left, right):
    return lax.dot_general(left, right, (((1,), (1,)), ((), ())), preferred_element_type=F32)


def at_layer(ref, layer):
    return ref.at[pl.ds(layer, 1)]


def turn(matrix):
    return matrix.astype(F32).T.astype(matrix.dtype)


def wide(column, lanes):
    return jnp.concatenate([column] * (lanes // WIDTH), axis=1)


def fold_lanes(values):
    total = values[:, :WIDTH]
    for start in range(WIDTH, values.shape[1], WIDTH):
        total = total + values[:, start : start + WIDTH]
    return total


def fold_heads(values):
    return jnp.concatenate([values] * (GROUP_LANES // WIDTH), axis=1)


def side_masks():
    lane = lax.broadcasted_iota(jnp.int32, (WIDTH, PAIR), 1)
    row = lax.broadcasted_iota(jnp.int32, (WIDTH, PAIR), 0)
    left = lane < PATCHES
    even = (row // HEAD_DIM) % 2 == 0
    return left, even


def token_mask(valid):
    return jnp.broadcast_to(valid, (WIDTH, valid.shape[1])).T


def shown_keys(keys, mask):
    parts = []
    for start in range(0, keys.shape[0], PATCHES):
        own = keys[start : start + PATCHES]
        parts.append(jnp.where(mask[start : start + PATCHES] > 0.5, own, own[PATCHES - 1 :]))
    return jnp.concatenate(parts, axis=0)


def spread_pair(tile, left, even, target):
    turned = pltpu.roll(tile, PATCHES, 1)
    keep = left == even
    first = jnp.where(keep, jnp.where(even, tile, turned), 0.0).astype(BF16)
    second = jnp.where(keep, jnp.where(even, turned, tile), 0.0).astype(BF16)
    step = 2 * HEAD_DIM
    for index in range(HEADS // 2):
        rows = slice(index * step, (index + 1) * step)
        lanes = slice(index * PAIR, (index + 1) * PAIR)
        target[0, rows, lanes] = first[rows]
        target[1, rows, lanes] = second[rows]


def halves(tile, left):
    return (
        jnp.where(left, tile, 0.0).astype(BF16),
        jnp.where(left, 0.0, tile).astype(BF16),
    )


def gather_heads(first, second, left):
    parts = []
    for head in range(HEADS // GROUPS):
        rows = slice(head * HEAD_DIM, (head + 1) * HEAD_DIM)
        lanes = slice(head // 2 * PAIR, (head // 2 + 1) * PAIR)
        one, two = first[rows, lanes], second[rows, lanes]
        if head % 2 == 0:
            two = pltpu.roll(two, PATCHES, 1)
        else:
            one = pltpu.roll(one, PATCHES, 1)
        parts.append(jnp.where(left[:HEAD_DIM], one, two))
    return jnp.concatenate(parts, axis=0)


def pair_lanes(pair):
    start = pair * PAIR
    return pl.ds(start if isinstance(start, int) else pl.multiple_of(start, PAIR), PAIR)


def pipeline(pairs, slots, score, soften, mix):
    even, odd = slots
    score(0, even)

    def two_pairs(index, carry):
        first = 2 * index
        mix(jnp.maximum(first - 1, 0), odd)
        score(first + 1, odd)
        soften(first, even)
        mix(first, even)
        score(jnp.minimum(first + 2, pairs - 1), even)
        soften(first + 1, odd)
        return carry

    lax.fori_loop(0, pairs // 2, two_pairs, 0, unroll=True)
    mix(pairs - 1, odd)


def chunks(lanes, work):
    for start in range(0, lanes, CHUNK):
        work(slice(start, start + CHUNK))


def each(count, work):
    if count == 1:
        work(0)
        return

    def one(index, carry):
        work(index)
        return carry

    lax.fori_loop(0, count, one, 0)


def device_at(index, sizes):
    return index // sizes[1], lax.rem(index, sizes[1])


def greet(step, sizes):
    others = sizes[0] * sizes[1]
    own = lax.axis_index("dp") * sizes[1] + lax.axis_index("patch")
    barrier = pltpu.get_barrier_semaphore()

    @pl.when(step == 0)
    def _():
        def signal(offset, carry):
            target = device_at(lax.rem(own + offset, others), sizes)
            pl.semaphore_signal(
                barrier, inc=1, device_id=target, device_id_type=pl.DeviceIdType.MESH
            )
            return carry

        lax.fori_loop(1, others, signal, 0)


def met(sizes):
    pl.semaphore_wait(pltpu.get_barrier_semaphore(), sizes[0] * sizes[1] - 1)


def second_step():
    return jnp.minimum(1, pl.num_programs(0) - 1)


def swap_tiles(sizes, tiles, send, arrive, meanwhile=None):
    others = sizes[0] * sizes[1]
    own = lax.axis_index("dp") * sizes[1] + lax.axis_index("patch")

    def start(offset, carry):
        pltpu.make_async_remote_copy(
            src_ref=tiles.at[own],
            dst_ref=tiles.at[own],
            send_sem=send,
            recv_sem=arrive,
            device_id=device_at(lax.rem(own + offset, others), sizes),
            device_id_type=pl.DeviceIdType.MESH,
        ).start()
        return carry

    lax.fori_loop(1, others, start, 0)
    if meanwhile is not None:
        meanwhile()
    await_bytes(tiles.at[pl.ds(0, others - 1)], arrive)
    await_bytes(tiles.at[pl.ds(0, others - 1)], send)


def await_bytes(like, sem):
    pltpu.make_async_copy(like, like, sem).wait()


def readout_copy(source, target, sems):
    return pltpu.make_async_remote_copy(
        src_ref=source,
        dst_ref=target,
        send_sem=sems.at[0],
        recv_sem=sems.at[1],
        device_id=(lax.axis_index("dp"), 1 - lax.axis_index("patch")),
        device_id_type=pl.DeviceIdType.MESH,
    )


def own_part(sizes, inner):
    chip = lax.axis_index("dp")
    return chip // inner, lax.rem(chip, inner) * sizes[1] + lax.axis_index("patch")


def first_patch(sizes, inner, patches, place):
    half = lax.rem(place + lax.axis_index("patch"), sizes[1])
    return (half * inner + place // sizes[1]) * (patches // (inner * sizes[1]))


class Spread:
    def __init__(self, sizes, inner, source, target, like, send, arrive, pieces=1):
        self.sizes, self.inner, self.pieces = sizes, inner, pieces
        self.source, self.target, self.like = source, target, like
        self.send, self.arrive = send, arrive
        self.devices = inner * sizes[1]
        self.group, self.own = own_part(sizes, inner)

    def start(self):
        def piece(ref, index):
            size = ref.shape[0] // self.pieces
            return ref if self.pieces == 1 else ref.at[pl.ds(index * size, size)]

        def begin(count, carry):
            index = (count - 1) // (self.devices - 1)
            offset = count - index * (self.devices - 1)
            other = lax.rem(self.own + offset, self.devices)
            pltpu.make_async_remote_copy(
                src_ref=piece(self.source(other), index),
                dst_ref=piece(self.target(self.own), index),
                send_sem=self.send,
                recv_sem=self.arrive,
                device_id=(
                    self.group * self.inner + other // self.sizes[1],
                    lax.rem(other, self.sizes[1]),
                ),
                device_id_type=pl.DeviceIdType.MESH,
            ).start()
            return carry

        pltpu.make_async_copy(
            self.source(self.own), self.target(self.own), self.arrive
        ).start()
        lax.fori_loop(1, self.pieces * (self.devices - 1) + 1, begin, 0)

    def receive(self):
        await_bytes(self.like(self.devices), self.arrive)

    def drain(self):
        await_bytes(self.like(self.devices - 1), self.send)

    def finish(self):
        self.receive()
        self.drain()


class Sharing:
    def __init__(self, sizes, inner, whole, source, slots, share, target, sems):
        rows = slots.shape[1]
        self.whole, self.source, self.slots, self.share = whole, source, slots, share

        def part(ref, place):
            return ref.at[pl.ds(pl.multiple_of(place * rows, rows), rows)]

        self.stages = [
            Spread(
                sizes,
                inner,
                lambda place: part(source, place),
                lambda place: slots.at[place],
                lambda count: slots.at[pl.ds(0, count)],
                sems.at[0, 0],
                sems.at[0, 1],
            ),
            Spread(
                sizes,
                inner,
                lambda place: share,
                lambda place: part(target, place),
                lambda count: target.at[pl.ds(0, rows * count)],
                sems.at[1, 0],
                sems.at[1, 1],
            ),
        ]

    def begin(self):
        self.source[...] = self.whole[...].astype(self.source.dtype)
        self.stages[0].start()

    def add(self):
        total = self.slots[0].astype(F32)
        for place in range(1, self.slots.shape[0]):
            total = total + self.slots[place].astype(F32)
        self.share[...] = total.astype(self.share.dtype)


def sharing_dtype(devices):
    return BF16 if 4 * WIDTH // devices % 16 == 0 else F32


def sharing_scratch(devices):
    rows = 4 * WIDTH // devices
    dtype = sharing_dtype(devices)
    return [
        pltpu.VMEM((4 * WIDTH, WIDTH), dtype),
        pltpu.VMEM((devices, rows, WIDTH), dtype),
        pltpu.VMEM((rows, WIDTH), dtype),
        pltpu.SemaphoreType.DMA((2, 2)),
    ]


def ship_rows(sizes, inner, flat, start, slots, send, arrive):
    patches = flat.shape[0]
    part, count = slots.shape[1:3]
    return Spread(
        sizes,
        inner,
        lambda place: flat.at[
            pl.ds(first_patch(sizes, inner, patches, place), part), pl.ds(start, count)
        ],
        lambda slot: slots.at[slot],
        lambda places: slots.at[pl.ds(0, places)],
        send,
        arrive,
        part,
    )


class Partner:
    def __init__(self, sizes, inner, partial, got, sems):
        chip = lax.axis_index("dp")
        self.half = lax.rem(chip, inner) // (inner // 2)
        self.other = chip + (1 - 2 * self.half) * (inner // 2)
        self.partial, self.got, self.sems = partial, got, sems

    def start(self):
        rows = self.got.shape[0]
        runs = math.gcd(rows // 16, 3) if rows % 16 == 0 else 1
        for run in range(runs):
            part = pl.ds(run * (rows // runs), rows // runs)
            pltpu.make_async_remote_copy(
                src_ref=self.partial.at[1 - self.half, part],
                dst_ref=self.got.at[part],
                send_sem=self.sems.at[0],
                recv_sem=self.sems.at[1],
                device_id=(self.other, lax.axis_index("patch")),
                device_id_type=pl.DeviceIdType.MESH,
            ).start()

    def wait(self):
        await_bytes(self.got, self.sems.at[1])
        await_bytes(self.got, self.sems.at[0])


def as_columns(row):
    return jnp.broadcast_to(row, (WIDTH, WIDTH)).T


def norm_stats(step, sizes, values, valid, gains, out, scratch):
    pivot, sums, squares, count, tiles, send, arrive = scratch
    lanes = valid.shape[-1]

    @pl.when(step == 0)
    def _():
        own = jnp.sum(valid[0])
        first = jnp.sum(fold_lanes(values[0] * valid[0]), axis=1, keepdims=True) / own
        pivot[...] = jnp.broadcast_to(first, (WIDTH, WIDTH))
        sums[...] = jnp.zeros_like(sums)
        squares[...] = jnp.zeros_like(squares)
        count[...] = jnp.zeros_like(count)

    def add(index, at):
        centred = (values[index, :, at] - wide(pivot[...], CHUNK)) * valid[index, :, at]
        sums[...] += fold_lanes(centred)
        squares[...] += fold_lanes(centred * centred)
        count[...] += jnp.broadcast_to(fold_lanes(valid[index, :, at]), count.shape)

    each(values.shape[0], lambda index: chunks(lanes, functools.partial(add, index)))

    @pl.when(step == pl.num_programs(0) - 1)
    def _():
        own = lax.axis_index("dp") * sizes[1] + lax.axis_index("patch")
        total = jnp.broadcast_to(jnp.sum(count[0:1, :]), (1, WIDTH))
        shift = jnp.sum(sums[...].T, axis=0, keepdims=True)
        square = jnp.sum(squares[...].T, axis=0, keepdims=True)
        tiles[own, 0:1, :] = pivot[...].T[0:1, :] + shift / total
        tiles[own, 1:2, :] = square - shift * shift / total
        tiles[own, 2:3, :] = total
        tiles[own, 3:4, :] = total

        def known():
            out[3] = as_columns(gains[1])
            out[5] = as_columns(gains[0])

        swap_tiles(sizes, tiles, send, arrive, known)
        means, spreads, counts = tiles[:, 0, :], tiles[:, 1, :], tiles[:, 2, :]
        total = jnp.sum(counts, axis=0, keepdims=True)
        mean = jnp.sum(means * counts, axis=0, keepdims=True) / total
        apart = means - mean
        variance = jnp.sum(spreads + counts * (apart * apart), axis=0, keepdims=True) / total
        inverse = lax.rsqrt(variance + EPS)
        out[0] = as_columns(mean)
        out[1] = as_columns(inverse)
        out[2] = as_columns(inverse * gains[0])
        out[4] = as_columns(total)


def add_gradient(grad, normal, valid, scratch):
    weighted = grad * valid
    scratch[0][...] += fold_lanes(weighted * normal)
    scratch[1][...] += fold_lanes(weighted)


def clear_gradient(step, scratch):
    @pl.when(step == 0)
    def _():
        scratch[0][...] = jnp.zeros_like(scratch[0])
        scratch[1][...] = jnp.zeros_like(scratch[1])


def gradient_sums(step, sizes, columns, columns_out, rows_out, scratch):
    by_normal, plain, tiles, send, arrive = scratch

    @pl.when(step == pl.num_programs(0) - 1)
    def _():
        own = lax.axis_index("dp") * sizes[1] + lax.axis_index("patch")
        tiles[own, 0:1, :] = jnp.sum(by_normal[...].T, axis=0, keepdims=True)
        tiles[own, 1:2, :] = jnp.sum(plain[...].T, axis=0, keepdims=True)
        swap_tiles(sizes, tiles, send, arrive)
        summed = jnp.sum(tiles[...], axis=0)
        rows_out[...] = summed
        total = columns[4]
        columns_out[0] = as_columns(summed[0:1, :]) / total
        columns_out[1] = as_columns(summed[1:2, :]) / total


def apply_norm(values, columns):
    lanes = values.shape[1]
    return (values - wide(columns[0], lanes)) * wide(columns[2], lanes) + wide(columns[3], lanes)


def normalise(values, columns):
    lanes = values.shape[1]
    return (values - wide(columns[0], lanes)) * wide(columns[1], lanes)


def back_norm(grad, normal, valid, columns, back_columns):
    lanes = grad.shape[1]
    inner = wide(back_columns[1], lanes) + normal * wide(back_columns[0], lanes)
    return wide(columns[2], lanes) * (grad - valid * inner)


def attention_forward_body(sizes, layer, first_layer, makes_head, *refs):
    if first_layer:
        x_ref, readout, refs = refs[0], refs[1], refs[2:]
        columns = None
    else:
        x_ref, columns, refs = refs[0], refs[1], refs[2:]
    w_in_ref, w_out_ref, valid_ref, scales, offsets = refs[:5]
    refs = refs[5:]
    if makes_head:
        head_refs, refs = refs[:3], refs[3:]
    h_out, qkv_out, o_out, lse_out, columns_out = refs[:5]
    refs = refs[5:]
    if first_layer:
        readout_out, readout_sems = refs[0], refs[-1]
        refs = refs[1:-1]
    if makes_head:
        head_refs, refs = head_refs + refs[:1], refs[1:]
    size = len(FORWARD_SLOT)
    slots, refs = (refs[:size], refs[size : 2 * size]), refs[2 * size :]
    (x_full, q_full, k_rows, tops, sums, w_in, w_out), scratch = refs[:7], refs[7:]
    w_in_ref, w_out_ref = at_layer(w_in_ref, layer), at_layer(w_out_ref, layer)
    step = pl.program_id(0)
    greet(step, sizes)

    @pl.when(step == second_step())
    def _():
        met(sizes)
        if first_layer:
            readout_copy(readout, readout_out, readout_sems).start()

    lanes = h_out.shape[-1]
    pairs = lanes // PAIR

    @pl.when(step == 0)
    def _():
        for slot in slots:
            slot[0][...] = jnp.zeros_like(slot[0])
        for part in range(3):
            w_in[part * WIDTH : (part + 1) * WIDTH, :] = turn(w_in_ref[0, part])
        w_out[...] = turn(w_out_ref[0])

    if makes_head:
        head_backward(step, *head_refs)

    def project(at):
        x = x_ref[at, :].astype(F32).T if first_layer else apply_norm(x_ref[0, :, at], columns)
        x_full[:, at] = x
        low = x.astype(BF16)
        q = dot(w_in[0:WIDTH, :], low)
        q_full[:, at] = q
        qkv_out[0, 0:WIDTH, at] = q.astype(BF16)
        k = dot(w_in[WIDTH : 2 * WIDTH, :], low)
        k_rows[at, :] = shown_keys(k.T, token_mask(valid_ref[0, :, at])).astype(BF16)
        qkv_out[0, WIDTH : 2 * WIDTH, at] = k.astype(BF16)
        qkv_out[0, 2 * WIDTH :, at] = dot(w_in[2 * WIDTH :, :], low).astype(BF16)

    chunks(lanes, project)
    left, even = side_masks()

    def score(pair, slot):
        spread, scores, _ = slot
        at = pair_lanes(pair)
        spread_pair(q_full[:, at], left, even, spread)
        keys = k_rows[at, :]
        for side in range(2):
            own = slice(side * PATCHES, (side + 1) * PATCHES)
            for group in range(GROUPS):
                cut = slice(group * GROUP_LANES, (group + 1) * GROUP_LANES)
                scores[own, cut] = dot(keys[own], spread[side, :, cut])

    def soften(pair, slot):
        _, scores, weights = slot
        for side in range(2):
            own = slice(side * PATCHES, (side + 1) * PATCHES)
            for group in range(GROUPS):
                cut = slice(group * GROUP_LANES, (group + 1) * GROUP_LANES)
                shown = scores[own, cut]
                top = jnp.max(shown, axis=0, keepdims=True)
                weights[own, cut] = jnp.exp2((shown - top) * SCALE_LOG2).astype(BF16)
                tops[pl.ds(2 * pair + side, 1), cut] = top

    def mix(pair, slot):
        _, _, weights = slot
        at = pair_lanes(pair)
        valid = valid_ref[0, :, at]
        v_one, v_two = halves(qkv_out[0, 2 * WIDTH :, at].astype(F32) * valid, left)
        ones = jnp.broadcast_to(valid, (HEAD_DIM, PAIR))
        some = left[:HEAD_DIM]
        ones = jnp.concatenate([jnp.where(some, ones, 0.0), jnp.where(some, 0.0, ones)], axis=0)
        ones = ones.astype(BF16)
        for group in range(GROUPS):
            cut = slice(group * GROUP_LANES, (group + 1) * GROUP_LANES)
            rows = slice(group * GROUP_ROWS, (group + 1) * GROUP_ROWS)
            mixed = dot(
                jnp.concatenate([v_one[rows], v_two[rows], ones], axis=0), weights[:, cut]
            )
            products = []
            for side in range(2):
                start = 2 * GROUP_ROWS + side * HEAD_DIM
                total = mixed[start : start + HEAD_DIM]
                sums[pl.ds(2 * pair + side, 1), cut] = total[0:1]
                inverse = jnp.concatenate([1.0 / total] * (GROUP_ROWS // HEAD_DIM), axis=0)
                products.append(mixed[side * GROUP_ROWS : (side + 1) * GROUP_ROWS] * inverse)
            o_out[0, rows, at] = gather_heads(*products, left).astype(BF16)

    pipeline(pairs, slots, score, soften, mix)
    lse_out[0] = tops[...] * SCALE_LOG2 + jnp.log2(sums[...])

    def attend(at):
        h_out[0, :, at] = x_full[:, at] + dot(w_out[...], o_out[0, :, at])

    chunks(lanes, attend)
    if first_layer:

        @pl.when(step == pl.num_programs(0) - 1)
        def _():
            readout_copy(readout, readout_out, readout_sems).wait()

    gains = scales[layer, 0:1, :], offsets[layer, 0:1, :]
    norm_stats(step, sizes, h_out, valid_ref, gains, columns_out, scratch)


def feed_forward_body(
    sizes, layer, h_ref, columns, w_up_ref, w_down_ref, valid_ref, scales, offsets,
    f_out, columns_out, w_up, w_down, *scratch,
):
    w_up_ref, w_down_ref = at_layer(w_up_ref, layer), at_layer(w_down_ref, layer)
    step = pl.program_id(0)
    greet(step, sizes)

    @pl.when(step == second_step())
    def _():
        met(sizes)

    @pl.when(step == 0)
    def _():
        w_up[...] = turn(w_up_ref[0])
        w_down[...] = turn(w_down_ref[0])

    def feed(index, at):
        normed = apply_norm(h_ref[index, :, at], columns)
        u = dot(w_up[...], normed.astype(BF16)).astype(BF16).astype(F32)
        bent = jnp.tanh(u * (GELU_IN + (GELU_IN * GELU_CUBE) * (u * u)))
        half = 0.5 * u
        active = (half + half * bent).astype(BF16)
        f_out[index, :, at] = normed + dot(w_down[...], active)

    each(h_ref.shape[0], lambda index: chunks(h_ref.shape[-1], functools.partial(feed, index)))
    gains = scales[layer, 1:2, :], offsets[layer, 1:2, :]
    norm_stats(step, sizes, f_out, valid_ref, gains, columns_out, scratch)


def turn_body(
    sizes, inner, f_ref, columns, valid_ref, gz_ref, flat_out, gx_out, back_out, rows_out,
    slots_out, turned, sent, row_sems, *scratch,
):
    step = pl.program_id(0)
    patches, block = gz_ref.shape[:2]
    part = slots_out.shape[1]
    early = sent.shape[0]
    greet(step, sizes)

    def shipment(index):
        return Spread(
            sizes,
            inner // 2,
            lambda place: sent.at[
                index, pl.ds(first_patch(sizes, inner // 2, patches, place), part)
            ],
            lambda slot: slots_out.at[
                slot, :, pl.ds(pl.multiple_of(index * block, block), block)
            ],
            lambda places: slots_out.at[pl.ds(0, places), :, pl.ds(0, block)],
            row_sems.at[0, index],
            row_sems.at[1, index],
        )

    @pl.when(step == second_step())
    def _():
        met(sizes)

    @pl.when((step >= 1) & (step <= early))
    def _():
        shipment(step - 1).start()

    clear_gradient(step, scratch)
    shift = lax.axis_index("patch") * (patches // sizes[1])

    def rows_at(patch):
        return pl.ds(lax.rem(patch + shift, patches), block, stride=patches)

    def show(at):
        turned[at, :] = (apply_norm(f_ref[0, :, at], columns) * valid_ref[0, :, at]).T

    def take(at):
        valid = valid_ref[0, :, at]
        grad = turned[at, :].T * valid
        gx_out[0, :, at] = grad
        add_gradient(grad, normalise(f_ref[0, :, at], columns), valid, scratch)

    chunks(f_ref.shape[-1], show)
    for patch in range(patches):
        flat_out[patch] = turned[rows_at(patch), :].astype(BF16)
    for patch in range(patches):
        turned[rows_at(patch), :] = gz_ref[patch]
    chunks(f_ref.shape[-1], take)

    @pl.when(step < early)
    def _():
        sent[step] = flat_out[...]

    @pl.when(step == pl.num_programs(0) - 1)
    def _():
        for index in range(early):
            shipment(index).finish()

    gradient_sums(step, sizes, columns, back_out, rows_out, scratch)


def head_backward(step, cotangent, readout_own, readout_other, out):
    def rows(readout):
        grad = dot(cotangent[...], readout[...])
        for patch in range(out.shape[0]):
            out[patch] = grad[:, patch * WIDTH : (patch + 1) * WIDTH]

    pl.when(step < READOUT_CHUNKS)(lambda: rows(readout_own))
    pl.when((step >= READOUT_CHUNKS) & (step < 2 * READOUT_CHUNKS))(lambda: rows(readout_other))


def head_forward(step, flat, readout_own, readout_other, out, total):
    @pl.when(step == 0)
    def _():
        total[...] = jnp.zeros_like(total)

    def rows(readout):
        for patch in range(0, flat.shape[0], 2):
            pair = jnp.concatenate([flat[patch], flat[patch + 1]], axis=1)
            total[...] += dot_rows(pair, readout[:, patch * WIDTH : (patch + 2) * WIDTH])

    pl.when(step < READOUT_CHUNKS)(lambda: rows(readout_own))
    pl.when((step >= READOUT_CHUNKS) & (step < 2 * READOUT_CHUNKS))(lambda: rows(readout_other))

    @pl.when(step == 2 * READOUT_CHUNKS - 1)
    def _():
        out[...] = total[...].astype(out.dtype)


def head_specs(horizon, half_rows, patches, series):
    chunk = half_rows // READOUT_CHUNKS
    last = 2 * READOUT_CHUNKS - 1
    flat_spec = pl.BlockSpec(
        (chunk // WIDTH, series, WIDTH), lambda step: (jnp.minimum(step, last), 0, 0)
    )
    own_spec = pl.BlockSpec(
        (horizon, chunk), lambda step: (0, jnp.minimum(step, READOUT_CHUNKS - 1))
    )
    other_spec = pl.BlockSpec(
        (horizon, chunk),
        lambda step: (0, jnp.clip(step - READOUT_CHUNKS, 0, READOUT_CHUNKS - 1)),
    )
    return flat_spec, own_spec, other_spec


def head_gradient_body(half, *refs):
    *parts, cotangent, out, total = refs
    step = pl.program_id(0)

    @pl.when(step == 0)
    def _():
        total[...] = jnp.zeros_like(total)

    sources, part, _, width = parts[0].shape
    start = 0
    for rows in parts:
        count = rows.shape[2]
        right = cotangent[:, start : start + count].reshape(sources * count, -1)
        start += count
        for patch in range(part):
            left = rows[:, patch].reshape(sources * count, width)
            total[patch] += lax.dot_general(
                left, right, (((0,), (0,)), ((), ())), preferred_element_type=F32
            )

    @pl.when(step == pl.num_programs(0) - 1)
    def _():
        for patch in range(part):
            index, place = divmod(patch, part // 2)
            lanes = slice(place * width, (place + 1) * width)
            out[index, :, lanes] = total[patch].T.astype(out.dtype)


def widen_body(layers, *refs):
    rows, summed, *tiles = refs[: 2 + 2 * layers]
    out, in_out, out_out, up_out, down_out, gain_out, shift_out = refs[2 + 2 * layers :]
    width = rows.shape[-1]
    for at in range(2 * rows.shape[1]):
        out[:, at * width : (at + 1) * width] = rows[at % 2, at // 2].astype(out.dtype)

    @pl.when(pl.program_id(0) == 0)
    def _():
        for layer in range(layers):
            attention = 2 * (layers - layer) if layer else 0
            feed = 2 * (layers - layer) - 1
            out_out[layer] = summed[attention, 0:WIDTH, :].astype(F32)
            for part in range(3):
                rows_of_part = slice((part + 1) * WIDTH, (part + 2) * WIDTH)
                in_out[layer, part] = summed[attention, rows_of_part, :].astype(F32)
            up_out[layer, :, :WIDTH] = summed[feed, :WIDTH, :].astype(F32)
            up_out[layer, :, WIDTH:] = summed[feed, WIDTH : 2 * WIDTH, :].astype(F32)
            down_out[layer] = summed[feed, 2 * WIDTH :, :].astype(F32)
            for norm in range(2):
                tile = tiles[2 * layer + norm]
                gain_out[layer, norm : norm + 1, :] = tile[0:1, :]
                shift_out[layer, norm : norm + 1, :] = tile[1:2, :]


def feed_backward_body(sizes, inner, layer, ships, *refs):
    (gx_ref, f_ref, h_ref, columns_two, back_two, columns_one, w_down, w_up,
     valid_ref), refs = refs[:9], refs[9:]
    w_down, w_up = at_layer(w_down, layer), at_layer(w_up, layer)
    if ships:
        flat_chunk, readout_own, readout_other, flat, *refs = refs
        gy_out, weights_out, back_out, rows_out, out, slots_out, total, *scratch = refs
        scratch, row_sems = scratch[:-1], scratch[-1]
        rows_sent = ship_rows(
            sizes,
            inner // 2,
            flat,
            flat.shape[1] - slots_out.shape[2],
            slots_out,
            row_sems.at[0],
            row_sems.at[1],
        )
    else:
        gy_out, weights_out, back_out, rows_out, *scratch = refs
    step = pl.program_id(0)
    greet(step, sizes)

    @pl.when(step == second_step())
    def _():
        met(sizes)
        if ships:
            rows_sent.start()

    if ships:
        head_forward(step, flat_chunk, readout_own, readout_other, out, total)
    active_full, low_full, normed_full, units_full, w_up_turned, *scratch = scratch
    clear_gradient(step, scratch)

    @pl.when(step == 0)
    def _():
        weights_out[...] = jnp.zeros_like(weights_out)
        w_up_turned[...] = turn(w_up[0])

    def feed(at):
        valid = valid_ref[0, :, at]
        normed = apply_norm(h_ref[0, :, at], columns_one).astype(BF16)
        normed_full[:, at] = normed
        normal = normalise(f_ref[0, :, at], columns_two)
        grad = back_norm(gx_ref[0, :, at], normal, valid, columns_two, back_two)
        low = grad.astype(BF16)
        low_full[:, at] = low
        grad_units = []
        for start in range(0, w_down.shape[1], WIDTH):
            rows = slice(start, start + WIDTH)
            u = dot(w_up_turned[rows, :], normed).astype(BF16).astype(F32)
            square = u * u
            bent = jnp.tanh(u * (GELU_IN + (GELU_IN * GELU_CUBE) * square))
            half = 0.5 + 0.5 * bent
            active_full[rows, at] = (u * half).astype(BF16)
            inner = (0.5 * GELU_IN) + (1.5 * GELU_IN * GELU_CUBE) * square
            slope = half + (u * inner) * (1.0 - bent * bent)
            grad_units.append((dot(w_down[0, rows, :], low) * slope).astype(BF16))
            units_full[rows, at] = grad_units[-1]
        normal = normalise(h_ref[0, :, at], columns_one)
        grad_normed = grad + dot(w_up[0], jnp.concatenate(grad_units, axis=0))
        gy_out[0, :, at] = grad_normed
        add_gradient(grad_normed, normal, valid, scratch)

    chunks(gx_ref.shape[-1], feed)
    weights_out[2 * WIDTH :, :] += dot_rows(active_full[...], low_full[...])
    by_up = dot_rows(normed_full[...], units_full[...])
    weights_out[0:WIDTH, :] += by_up[:, :WIDTH]
    weights_out[WIDTH : 2 * WIDTH, :] += by_up[:, WIDTH:]
    if ships:
        pl.when(step == pl.num_programs(0) - 1)(rows_sent.finish)
    gradient_sums(step, sizes, columns_one, back_out, rows_out, scratch)


def attention_backward_body(sizes, inner, layer, opens, closes, start, *refs):
    first_layer = layer == 0
    (gy_ref, h_ref, qkv_ref, o_ref, lse_ref, valid_ref, columns_one, back_one, w_out, w_in_ref,
     x_ref), refs = refs[:11], refs[11:]
    w_out, w_in_ref = at_layer(w_out, layer), at_layer(w_in_ref, layer)
    taken = made = None
    if first_layer:
        ready, (gx_out, summed_out), refs = refs[:3], refs[3:5], refs[5:]
        arrays = 1 + len(ready)
        each = len(sharing_scratch(inner * sizes[1]))
        refs, weights_out, shared = (
            refs[: -1 - each * arrays],
            refs[-1 - each * arrays],
            refs[-each * arrays :],
        )
        shares = []
        for at, whole in enumerate((weights_out,) + tuple(ready)):
            source, slots, share, sems = shared[each * at : each * (at + 1)]
            shares.append(
                Sharing(sizes, inner, whole, source, slots, share, summed_out.at[at], sems)
            )
    else:
        columns_prev, *refs = refs
        if start:
            partial, *refs = refs
        if not opens:
            _, taken, *refs = refs
            taken, made = (taken, refs[0]), None
            refs = refs[1:]
        if closes:
            gx_out, weights_out, back_out, rows_out, *refs = refs
        else:
            gx_out, weights_out, made, *refs = refs
        if start:
            rows_out, *refs, got, row_sems = refs
            partner = Partner(sizes, inner, partial, got, row_sems)
        count = len(SUM_SCRATCH) + len(swap_scratch(sizes, 2))
        refs, scratch = refs[:-count], refs[-count:]
    size = len(BACKWARD_SLOT)
    slots = refs[:size], refs[size : 2 * size]
    low_full, grad_full, g_full, k_rows, v_rows, grads, w_in = refs[2 * size :]
    step = pl.program_id(0)
    last = pl.num_programs(0) - 1
    if closes or start:
        greet(step, sizes)

        @pl.when(step == second_step())
        def _():
            met(sizes)
            if first_layer:
                for share in shares[1:]:
                    share.begin()
            elif start:
                partner.start()

    if first_layer:

        @pl.when(step == jnp.maximum(second_step(), last // 2 + 1))
        def _():
            for share in shares[1:]:
                share.stages[0].receive()
                share.add()
                share.stages[1].start()

    lanes = valid_ref.shape[-1]
    pairs = lanes // PAIR

    @pl.when(step == 0)
    def _():
        for slot in slots:
            slot[0][...] = jnp.zeros_like(slot[0])
            slot[1][...] = jnp.zeros_like(slot[1])
        weights_out[...] = jnp.zeros_like(weights_out) if taken is None else taken[0][...]
        for part in range(3):
            w_in[:, part * WIDTH : (part + 1) * WIDTH] = w_in_ref[0, part]

    if not first_layer and taken is None:
        clear_gradient(step, scratch)
    elif not first_layer:

        @pl.when(step == 0)
        def _():
            scratch[0][...] = taken[1][0]
            scratch[1][...] = taken[1][1]

    def prepare(at):
        normal = normalise(h_ref[0, :, at], columns_one)
        grad = back_norm(gy_ref[0, :, at], normal, valid_ref[0, :, at], columns_one, back_one)
        grad_full[:, at] = grad
        low = grad.astype(BF16)
        low_full[:, at] = low
        g_full[:, at] = dot(w_out[0], low).astype(BF16).astype(F32)
        mask = token_mask(valid_ref[0, :, at])
        keys = shown_keys(qkv_ref[0, WIDTH : 2 * WIDTH, at].astype(F32).T, mask)
        k_rows[at, :] = keys.astype(BF16)
        v_rows[at, :] = (qkv_ref[0, 2 * WIDTH :, at].astype(F32).T * mask).astype(BF16)

    chunks(lanes, prepare)
    weights_out[0:WIDTH, :] += dot_rows(o_ref[0], low_full[...])
    left, even = side_masks()

    def score(pair, slot):
        spread_q, spread_g, scores, pulls, _, _, inner = slot
        at = pair_lanes(pair)
        spread_pair(qkv_ref[0, 0:WIDTH, at].astype(F32), left, even, spread_q)
        grad = g_full[:, at]
        spread_pair(grad, left, even, spread_g)
        keys = k_rows[at, :]
        content = v_rows[at, :]
        for side in range(2):
            own = slice(side * PATCHES, (side + 1) * PATCHES)
            for group in range(GROUPS):
                cut = slice(group * GROUP_LANES, (group + 1) * GROUP_LANES)
                scores[own, cut] = dot(keys[own], spread_q[side, :, cut])
                pulls[own, cut] = dot(content[own], spread_g[side, :, cut])
        products = grad * o_ref[0, :, at].astype(F32)
        some = left[:HEAD_DIM]
        for head in range(0, HEADS, 2):
            both = [
                jnp.broadcast_to(
                    jnp.sum(products[start : start + HEAD_DIM], axis=0, keepdims=True),
                    (HEAD_DIM, PAIR),
                )
                for start in (head * HEAD_DIM, (head + 1) * HEAD_DIM)
            ]
            turned = [pltpu.roll(row, PATCHES, 1) for row in both]
            lanes_of = slice(head * PATCHES, (head + 2) * PATCHES)
            inner[0, :, lanes_of] = jnp.where(some, both[0], turned[1])
            inner[1, :, lanes_of] = jnp.where(some, turned[0], both[1])

    def soften(pair, slot):
        _, _, scores, pulls, weights, slopes, inner = slot
        for side in range(2):
            own = slice(side * PATCHES, (side + 1) * PATCHES)
            for group in range(GROUPS):
                cut = slice(group * GROUP_LANES, (group + 1) * GROUP_LANES)
                total = lse_ref[0, pl.ds(2 * pair + side, 1), cut]
                weight = jnp.exp2(scores[own, cut] * SCALE_LOG2 - total)
                weights[own, cut] = weight.astype(BF16)
                mean = jnp.concatenate([inner[side, :, cut]] * (PATCHES // HEAD_DIM), axis=0)
                slopes[own, cut] = (weight * (pulls[own, cut] - mean)).astype(BF16)

    def mix(pair, slot):
        spread_q, spread_g, _, _, weights, slopes, _ = slot
        at = pair_lanes(pair)
        valid = valid_ref[0, :, at]
        k_one, k_two = halves(qkv_ref[0, WIDTH : 2 * WIDTH, at].astype(F32) * valid, left)
        own_left = left[:GROUP_ROWS]
        for group in range(GROUPS):
            cut = slice(group * GROUP_LANES, (group + 1) * GROUP_LANES)
            start = group * GROUP_ROWS
            rows = slice(start, start + GROUP_ROWS)
            weight = weights[:, cut]
            slope = slopes[:, cut]
            by_value = dot_rows(
                jnp.concatenate([spread_g[0, rows, cut], spread_g[1, rows, cut]], axis=0), weight
            )
            by_value = jnp.where(own_left, by_value[:GROUP_ROWS], by_value[GROUP_ROWS:])
            grads[2 * WIDTH + start : 2 * WIDTH + start + GROUP_ROWS, at] = (
                by_value * valid
            ).astype(BF16)
            by_key = dot_rows(
                jnp.concatenate([spread_q[0, rows, cut], spread_q[1, rows, cut]], axis=0), slope
            )
            by_key = jnp.where(own_left, by_key[:GROUP_ROWS], by_key[GROUP_ROWS:])
            grads[WIDTH + start : WIDTH + start + GROUP_ROWS, at] = (
                by_key * (valid * SCALE)
            ).astype(BF16)
            by_query = dot(jnp.concatenate([k_one[rows], k_two[rows]], axis=0), slope)
            grads[rows, at] = (
                gather_heads(by_query[:GROUP_ROWS], by_query[GROUP_ROWS:], left) * SCALE
            ).astype(BF16)

    pipeline(pairs, slots, score, soften, mix)

    def add_weights():
        for part in range(3):
            rows = slice(part * WIDTH, (part + 1) * WIDTH)
            weights_out[(part + 1) * WIDTH : (part + 2) * WIDTH, :] += dot_rows(
                low_full[...], grads[rows, :]
            )

    if first_layer:
        low_full[...] = x_ref[...].astype(F32).T.astype(BF16)
        add_weights()
        pl.when(step == last)(shares[0].begin)

    def finish(at):
        if not first_layer:
            normal = normalise(x_ref[0, :, at], columns_prev)
            inputs = normal * wide(columns_prev[5], CHUNK) + wide(columns_prev[3], CHUNK)
            low_full[:, at] = inputs.astype(BF16)
        grad = grad_full[:, at] + dot(w_in[...], grads[:, at])
        if first_layer:
            gx_out[at, :] = grad.T.astype(BF16)
        else:
            gx_out[0, :, at] = grad
            add_gradient(grad, normal, valid_ref[0, :, at], scratch)

    chunks(lanes, finish)
    if not first_layer:
        add_weights()
    if first_layer:

        @pl.when(step == last)
        def _():
            for share in shares[1:]:
                share.stages[0].drain()
                share.stages[1].finish()
            shares[0].stages[0].receive()
            shares[0].add()
            shares[0].stages[1].start()
            shares[0].stages[0].drain()
            shares[0].stages[1].finish()

    else:
        if start:

            @pl.when(step == last)
            def _():
                partner.wait()
                total = partial[partner.half].astype(F32) + got[...].astype(F32)
                rows_out[...] = total.astype(rows_out.dtype)

        if closes:
            gradient_sums(step, sizes, columns_prev, back_out, rows_out, scratch)
        else:

            @pl.when(step == last)
            def _():
                made[0] = scratch[0][...]
                made[1] = scratch[1][...]


def fixed(shape):
    return pl.BlockSpec(memory_space=pltpu.VMEM)


def blocked(array, first=0):
    return pl.BlockSpec((1,) + array.shape[1:], lambda step: (first + step, 0, 0))


def grouped(array, group):
    return pl.BlockSpec((group,) + array.shape[1:], lambda step: (step, 0, 0))


def rows_of(lanes):
    return pl.BlockSpec((lanes, WIDTH), lambda step: (step, 0))


ANY = pl.BlockSpec(memory_space=pl.ANY)


def shaped(shape, dtype=F32):
    return jax.ShapeDtypeStruct(shape, dtype)


def call(
    body, blocks, ins, in_specs, outs, out_specs, scratch, flops, collective=None, aliases=None
):
    arrays = list(ins) + (list(outs) if isinstance(outs, tuple) else [outs])
    size = sum(math.prod(a.shape) * a.dtype.itemsize for a in arrays)
    return pl.pallas_call(
        body,
        grid=(blocks,),
        in_specs=in_specs,
        out_specs=out_specs,
        out_shape=outs,
        scratch_shapes=scratch,
        input_output_aliases=aliases or {},
        compiler_params=pltpu.CompilerParams(
            dimension_semantics=("arbitrary",),
            vmem_limit_bytes=VMEM_BYTES,
            collective_id=collective,
            has_side_effects=collective is not None,
        ),
        cost_estimate=pl.CostEstimate(flops=flops, bytes_accessed=size, transcendentals=0),
    )(*ins)


STAT_SCRATCH = [
    pltpu.VMEM((WIDTH, WIDTH), F32),
    pltpu.VMEM((WIDTH, WIDTH), F32),
    pltpu.VMEM((WIDTH, WIDTH), F32),
    pltpu.VMEM((8, WIDTH), F32),
]
FORWARD_SLOT = [
    pltpu.VMEM((2, WIDTH, SPREAD), BF16),
    pltpu.VMEM((PAIR, SPREAD), F32),
    pltpu.VMEM((PAIR, SPREAD), BF16),
]
BACKWARD_SLOT = [
    pltpu.VMEM((2, WIDTH, SPREAD), BF16),
    pltpu.VMEM((2, WIDTH, SPREAD), BF16),
    pltpu.VMEM((PAIR, SPREAD), F32),
    pltpu.VMEM((PAIR, SPREAD), F32),
    pltpu.VMEM((PAIR, SPREAD), BF16),
    pltpu.VMEM((PAIR, SPREAD), BF16),
    pltpu.VMEM((2, HEAD_DIM, SPREAD), F32),
]
SUM_SCRATCH = [pltpu.VMEM((WIDTH, WIDTH), F32), pltpu.VMEM((WIDTH, WIDTH), F32)]


def swap_scratch(sizes, rows):
    devices = sizes[0] * sizes[1]
    return [
        pltpu.VMEM((devices, rows, WIDTH), F32),
        pltpu.SemaphoreType.DMA,
        pltpu.SemaphoreType.DMA,
    ]


def head_gradient(sizes, inner, parts, batch_cotangent):
    sources, part, _, width = parts[0].shape
    series, horizon = batch_cotangent.shape[1:]
    half = lax.axis_index("dp") // (inner // 2)
    at_once = 4
    steps = sources // at_once
    return pl.pallas_call(
        head_gradient_body,
        grid_spec=pltpu.PrefetchScalarGridSpec(
            num_scalar_prefetch=1,
            grid=(steps,),
            in_specs=[
                pl.BlockSpec((at_once,) + rows.shape[1:], lambda step, half: (step, 0, 0, 0))
                for rows in parts
            ]
            + [
                pl.BlockSpec(
                    (at_once, series, horizon), lambda step, half: (half[0] * steps + step, 0, 0)
                )
            ],
            out_specs=pl.BlockSpec(memory_space=pltpu.VMEM),
            scratch_shapes=[pltpu.VMEM((part, width, horizon), F32)],
        ),
        out_shape=shaped((2, horizon, part // 2 * width), BF16),
        compiler_params=pltpu.CompilerParams(
            dimension_semantics=("arbitrary",), vmem_limit_bytes=VMEM_BYTES
        ),
        cost_estimate=pl.CostEstimate(
            flops=2 * sources * series * part * width * horizon,
            bytes_accessed=2 * sources * series * (part * width + horizon),
            transcendentals=0,
        ),
    )(half.astype(jnp.int32).reshape(1), *parts, batch_cotangent)


def spread_head(sizes, inner, rows):
    gathered = lax.all_gather(rows, "dp", axis=0)
    outer = sizes[0] // inner
    if outer > 1:
        gathered = jnp.sum(gathered.reshape((outer, inner) + rows.shape).astype(F32), axis=0)
    return gathered


def finish_outputs(rows, summed, tiles, layers, hidden):
    inner, horizon, columns = rows.shape
    rows = rows.reshape(2, inner // 2, horizon, columns)
    at_once = math.gcd(inner, 4)
    shapes = (
        shaped((horizon, inner * columns)),
        shaped((layers, 3, WIDTH, WIDTH)),
        shaped((layers, WIDTH, WIDTH)),
        shaped((layers, WIDTH, hidden)),
        shaped((layers, hidden, WIDTH)),
        shaped((layers, 2, WIDTH)),
        shaped((layers, 2, WIDTH)),
    )
    head, *others = call(
        functools.partial(widen_body, layers),
        inner // at_once,
        (rows, summed, *tiles),
        [
            pl.BlockSpec((2, at_once // 2, horizon, columns), lambda step: (0, step, 0, 0)),
            fixed(summed.shape),
        ]
        + [fixed(tile.shape) for tile in tiles],
        shapes,
        (pl.BlockSpec((horizon, at_once * columns), lambda step: (0, step)),)
        + tuple(fixed(shape.shape) for shape in shapes[1:]),
        [],
        1,
    )
    return *others, head.T


def per_device(
    sizes,
    embedded_segments,
    history_durations,
    segment_seen_indicator,
    query_key_value_matrices,
    mixing_result_matrices,
    first_dense_matrices,
    second_dense_matrices,
    batchnorm_scales,
    batchnorm_offsets,
    readout_matrix,
    prediction_cotangent,
):
    series, patches, width = embedded_segments.shape
    layers = query_key_value_matrices.shape[0]
    hidden = first_dense_matrices.shape[2]
    block = math.gcd(series, 16)
    blocks = series // block
    lanes = block * patches
    tokens = series * patches
    positions = jnp.arange(patches, dtype=jnp.int32)
    first_valid = patches - ((history_durations - 16) // 8 + 2)
    valid = (positions[None, :] >= first_valid[:, None]) & (segment_seen_indicator > 0)
    valid_rows = valid.astype(F32).reshape(blocks, 1, lanes)
    embedded = embedded_segments.reshape(tokens, width)
    horizon = readout_matrix.shape[1]
    readout_own = readout_matrix.T
    inner = math.gcd(sizes[0], patches // sizes[1])
    wide_f32 = shaped((blocks, width, lanes))
    columns_shape = shaped((6, WIDTH, WIDTH))
    back_shape = shaped((2, WIDTH, WIDTH))
    tile_shape = shaped((2, WIDTH))
    norm_specs = [fixed(batchnorm_scales.shape), fixed(batchnorm_offsets.shape)]
    half_rows = readout_matrix.shape[0]
    flat_spec, own_spec, other_spec = head_specs(horizon, half_rows, patches, series)
    pm_f32 = shaped((patches, series, width))
    pm_bf16 = shaped((patches, series, width), BF16)
    group = 3 if blocks % 3 == 0 else 1
    series_spec = pl.BlockSpec((patches, block, width), lambda step: (0, step, 0))
    weights_shape = shaped((4 * width, width))
    stat_swap, sum_swap = swap_scratch(sizes, 4), swap_scratch(sizes, 2)
    kept = []
    columns = None
    state = embedded
    batch_cotangent = lax.all_gather(prediction_cotangent, ("dp", "patch"), axis=0)
    for layer in range(layers):
        first = layer == 0
        qkv_shape = shaped((blocks, 3 * width, lanes), BF16)
        o_shape = shaped((blocks, width, lanes), BF16)
        lse_shape = shaped((blocks, block, SPREAD))
        ins = (state, readout_own) if first else (state, columns)
        specs = [rows_of(lanes), ANY] if first else [blocked(state), fixed(columns.shape)]
        makes_head = layer == layers - 1
        attended, qkv, mixed, lse, columns_one, *extra = call(
            functools.partial(attention_forward_body, sizes, layer, first, makes_head),
            blocks,
            ins
            + (
                query_key_value_matrices,
                mixing_result_matrices,
                valid_rows,
                batchnorm_scales,
                batchnorm_offsets,
            )
            + ((prediction_cotangent, readout_own, readout_other) if makes_head else ()),
            specs
            + [fixed(query_key_value_matrices.shape), fixed(mixing_result_matrices.shape)]
            + [blocked(valid_rows)]
            + norm_specs
            + (
                [fixed(prediction_cotangent.shape), own_spec, other_spec] if makes_head else []
            ),
            (wide_f32, qkv_shape, o_shape, lse_shape, columns_shape)
            + ((shaped(readout_own.shape, BF16),) if first else ())
            + ((pm_f32,) if makes_head else ()),
            (
                blocked(wide_f32),
                blocked(qkv_shape),
                blocked(o_shape),
                blocked(lse_shape),
                fixed(columns_shape.shape),
            )
            + ((ANY,) if first else ())
            + ((flat_spec,) if makes_head else ()),
            FORWARD_SLOT * 2
            + [
                pltpu.VMEM((width, lanes), F32),
                pltpu.VMEM((width, lanes), F32),
                pltpu.VMEM((lanes, width), BF16),
                pltpu.VMEM((block, SPREAD), F32),
                pltpu.VMEM((block, SPREAD), F32),
                pltpu.VMEM((3 * width, width), BF16),
                pltpu.VMEM((width, width), BF16),
            ]
            + STAT_SCRATCH
            + stat_swap
            + ([pltpu.SemaphoreType.DMA((2,))] if first else []),
            20 * 10**9,
            2 * layer,
        )
        if first:
            readout_other, *extra = extra
        if makes_head:
            (grad_rows,) = extra
        summed, columns_two = call(
            functools.partial(feed_forward_body, sizes, layer),
            blocks // group,
            (
                attended,
                columns_one,
                first_dense_matrices,
                second_dense_matrices,
                valid_rows,
                batchnorm_scales,
                batchnorm_offsets,
            ),
            [
                grouped(attended, group),
                fixed(columns_one.shape),
                fixed(first_dense_matrices.shape),
                fixed(second_dense_matrices.shape),
                grouped(valid_rows, group),
            ]
            + norm_specs,
            (wide_f32, columns_shape),
            (grouped(wide_f32, group), fixed(columns_shape.shape)),
            [pltpu.VMEM((hidden, width), BF16), pltpu.VMEM((width, hidden), BF16)]
            + STAT_SCRATCH
            + stat_swap,
            10 * 10**9,
            2 * layer + 1,
        )
        kept.append(
            (state, columns, attended, qkv, mixed, lse, columns_one, summed, columns_two)
        )
        state, columns = summed, columns_two

    sources = inner // 2 * sizes[1]
    early = max(4 * blocks // 9, 1)
    early_shape, late_shape = [
        shaped((sources, patches // sources, count, width), BF16)
        for count in (early * block, series - early * block)
    ]
    rows_shape = shaped((horizon, patches // sources // 2 * width), BF16)
    flat, grad_state, back_two, rows_two, early_rows = call(
        functools.partial(turn_body, sizes, inner),
        blocks,
        (state, columns, valid_rows, grad_rows),
        [blocked(state), fixed(columns.shape), blocked(valid_rows), series_spec],
        (pm_bf16, wide_f32, back_shape, tile_shape, early_shape),
        (
            series_spec,
            blocked(wide_f32),
            fixed(back_shape.shape),
            fixed(tile_shape.shape),
            ANY,
        ),
        [
            pltpu.VMEM((lanes, width), F32),
            pltpu.VMEM((early, patches, block, width), BF16),
            pltpu.SemaphoreType.DMA((2, early)),
        ]
        + SUM_SCRATCH
        + sum_swap,
        10**9,
        2 * layers,
    )
    out_shape = shaped((series, horizon), BF16)
    row_sems = [pltpu.SemaphoreType.DMA((2,))]

    weights, tiles = [], []
    for layer in reversed(range(layers)):
        first = layer == 0
        state, columns, attended, qkv, mixed, lse, columns_one, summed, columns_two = kept[layer]
        ships = layer == layers - 1
        grad_normed, feed_weights, back_one, rows_one, *extra = call(
            functools.partial(feed_backward_body, sizes, inner, layer, ships),
            blocks,
            (
                grad_state,
                summed,
                attended,
                columns_two,
                back_two,
                columns_one,
                second_dense_matrices,
                first_dense_matrices,
                valid_rows,
            )
            + ((flat, readout_own, readout_other, flat) if ships else ()),
            [
                blocked(grad_state),
                blocked(summed),
                blocked(attended),
                fixed(columns_two.shape),
                fixed(back_two.shape),
                fixed(columns_one.shape),
                fixed(second_dense_matrices.shape),
                fixed(first_dense_matrices.shape),
                blocked(valid_rows),
            ]
            + ([flat_spec, own_spec, other_spec, ANY] if ships else []),
            (wide_f32, weights_shape, back_shape, tile_shape)
            + ((out_shape, late_shape) if ships else ()),
            (
                blocked(wide_f32),
                fixed(weights_shape.shape),
                fixed(back_shape.shape),
                fixed(tile_shape.shape),
            )
            + ((fixed(out_shape.shape), ANY) if ships else ()),
            ([pltpu.VMEM(out_shape.shape, F32)] if ships else [])
            + [
                pltpu.VMEM((hidden, lanes), BF16),
                pltpu.VMEM((width, lanes), BF16),
                pltpu.VMEM((width, lanes), BF16),
                pltpu.VMEM((hidden, lanes), BF16),
                pltpu.VMEM((hidden, width), BF16),
            ]
            + SUM_SCRATCH
            + sum_swap
            + (row_sems if ships else []),
            20 * 10**9,
            2 * layers + 1 + 2 * layer,
        )
        if ships:
            predictions, late_rows = extra
            partial = head_gradient(sizes, inner, (early_rows, late_rows), batch_cotangent)
            grad_normed, partial = lax.optimization_barrier((grad_normed, partial))
        tiles = [rows_one, rows_two] + tiles
        scratch = BACKWARD_SLOT * 2 + [
            pltpu.VMEM((width, lanes), BF16),
            pltpu.VMEM((width, lanes), F32),
            pltpu.VMEM((width, lanes), F32),
            pltpu.VMEM((lanes, width), BF16),
            pltpu.VMEM((lanes, width), BF16),
            pltpu.VMEM((3 * width, lanes), BF16),
            pltpu.VMEM((width, 3 * width), BF16),
        ]
        ins = (
            grad_normed,
            attended,
            qkv,
            mixed,
            lse,
            valid_rows,
            columns_one,
            back_one,
            mixing_result_matrices,
            query_key_value_matrices,
            state,
        )

        def specs_from(at):
            return [
                blocked(grad_normed, at),
                blocked(attended, at),
                blocked(qkv, at),
                blocked(mixed, at),
                blocked(lse, at),
                blocked(valid_rows, at),
                fixed(columns_one.shape),
                fixed(back_one.shape),
                fixed(mixing_result_matrices.shape),
                fixed(query_key_value_matrices.shape),
            ]

        if first:
            others = tuple(weights) + (feed_weights,)
            devices = inner * sizes[1]
            summed_shape = shaped(
                (1 + len(others),) + weights_shape.shape, sharing_dtype(devices)
            )
            input_grad, summed_weights = call(
                functools.partial(attention_backward_body, sizes, inner, layer, True, True, False),
                blocks,
                ins + others,
                specs_from(0) + [rows_of(lanes)] + [fixed(weights_shape.shape)] * len(others),
                (shaped((tokens, width), BF16), summed_shape),
                (rows_of(lanes), ANY),
                scratch
                + [pltpu.VMEM(weights_shape.shape, F32)]
                + sharing_scratch(devices) * (1 + len(others)),
                50 * 10**9,
                2 * layers + 2 + 2 * layer,
            )
        else:
            cut = (blocks + 1) // 2 if ships else 0
            carried = ()
            if ships:
                grad_state, attention_weights, sums, head_rows = call(
                    functools.partial(
                        attention_backward_body, sizes, inner, layer, True, False, True
                    ),
                    cut,
                    ins + (columns, partial),
                    specs_from(0)
                    + [blocked(state), fixed(columns.shape), fixed(partial.shape)],
                    (wide_f32, weights_shape, back_shape, rows_shape),
                    (
                        blocked(wide_f32),
                        fixed(weights_shape.shape),
                        fixed(back_shape.shape),
                        fixed(rows_shape.shape),
                    ),
                    scratch
                    + SUM_SCRATCH
                    + sum_swap
                    + [pltpu.VMEM(rows_shape.shape, BF16)]
                    + row_sems,
                    25 * 10**9,
                    4 * layers + 1,
                )
                (*carried, grad_normed), head_rows = lax.optimization_barrier(
                    ((grad_state, attention_weights, sums, grad_normed), head_rows)
                )
                head_rows = spread_head(sizes, inner, head_rows)
            grad_state, attention_weights, back_two, rows_two = call(
                functools.partial(
                    attention_backward_body, sizes, inner, layer, not carried, True, False
                ),
                blocks - cut,
                (grad_normed,) + ins[1:] + (columns, *carried),
                specs_from(cut)
                + [blocked(state, cut), fixed(columns.shape)]
                + (
                    [ANY, fixed(weights_shape.shape), fixed(back_shape.shape)]
                    if carried
                    else []
                ),
                (wide_f32, weights_shape, back_shape, tile_shape),
                (
                    blocked(wide_f32, cut),
                    fixed(weights_shape.shape),
                    fixed(back_shape.shape),
                    fixed(tile_shape.shape),
                ),
                scratch + SUM_SCRATCH + sum_swap,
                25 * 10**9,
                2 * layers + 2 + 2 * layer,
                {len(ins) + 1: 0} if carried else None,
            )
            weights += [feed_weights, attention_weights]
    if devices < sizes[0] * sizes[1]:
        summed_weights = lax.psum(summed_weights.astype(F32), ("dp", "patch")) / devices
    return (
        predictions,
        input_grad.reshape(series, patches, width),
        *finish_outputs(head_rows, summed_weights, tiles, layers, hidden),
    )


def solution(mesh):
    placed = (
        P(("dp", "patch"), None, None),
        P(("dp", "patch")),
        P(("dp", "patch"), None),
        P(),
        P(),
        P(),
        P(),
        P(),
        P(),
        P("patch", None),
        P(("dp", "patch"), None),
    )
    sizes = (mesh.shape["dp"], mesh.shape["patch"])
    return jax.shard_map(
        functools.partial(per_device, sizes),
        mesh=mesh,
        in_specs=placed,
        out_specs=(
            P(("dp", "patch"), None),
            P(("dp", "patch"), None, None),
            P(),
            P(),
            P(),
            P(),
            P(),
            P(),
            P("patch", None),
        ),
        check_vma=False,
    )
```
